128 devices in a mesh: tm: 16 (over y, x_hi, core), space: 8 (over x_lo, z).
Axes of the slice: x: 4 (x_hi: 2, x_lo: 2; x = x_hi * 2 + x_lo), y: 4, z: 4, core: 2. Of those that a mesh axis runs over, the one named last changes fastest.
Arguments:
- starts: float32 [16, 64, 128, 128], P('tm', 'space'), may hold values from -6 to 6
- diffusivity: float32 [64, 128, 128], P('space'), may hold values from 0.04 to 0.2
- velocity: float32 [2, 64, 128, 128], P(None, 'space'), may hold values from -0.1 to 0.1
- obstacle: int32 [64, 128, 128], P('space'), may hold values from 0 to 1, as said below
- substep_scale: float32 [12], replicated, may hold values from 0.5 to 1
- neighbors: int32 [64, 4], P('space'), may hold values from 0 to 64, as said below
- coarse_x: float32 [64, 64, 64], P('space'), may hold values from -1 to 1
- coarse_y: float32 [64, 128, 128], P('space'), may hold values from -1 to 1
Outputs:
- slice_ends: float32 [16, 64, 128, 128], P('tm', 'space')
- increment: float32 [16, 64, 128, 128], P('tm', 'space')
The draws below stay inside these ranges and needn't reach their ends.
Inputs may be any that keep to these rules, and one draw needn't show every extreme that they name: `neighbors`: tiles form a grid of 8 by 8; each entry names the tile beside a tile in the given direction, or 64 on the grid's edge. The tiles 8 * k to 8 * (k + 1) - 1 fill grid row k, in any order within it, so a neighbour's number differs from the tile's block k by at most one block. `obstacle`: each tile holds one tube, a disc of radius 128 // 8 to 32 cells.
All inputs are finite; a program needn't handle non-finite values.
Results may differ from the reference program's by a relative error of at most 0.0002.
Values sent between devices are 32-bit elements; how exact they have to be, the bound alone decides.
A program may use at most 128 MiB of HBM per device.

```python
import math
import jax
import jax.numpy as jnp
from jax import lax

TILES_DEV = 8
TILE = 128
TGY = 8
SUB = 12
CX = 64
SLICES = 16
TILES = 64


def coarse_inverse(key, matrix_order):
    key_rate, key_mix = jax.random.split(key)
    low_rate = 0.2
    high_rate = 20.0
    rates = jnp.exp(jax.random.uniform(key_rate, (TILES, matrix_order), jnp.float32, math.log(low_rate), math.log(high_rate)))
    damping = 1.0 - 0.15 / math.sqrt(matrix_order)
    diagonal_part = jnp.exp(-rates / SLICES) * damping
    mixing = jax.random.uniform(key_mix, (TILES, matrix_order, matrix_order), jnp.float32, -1.0, 1.0)
    mixing = 0.15 * (mixing + jnp.swapaxes(mixing, 1, 2)) / (2.0 * matrix_order)
    identity_mask = jnp.eye(matrix_order, dtype=jnp.float32)
    return mixing * (1.0 - identity_mask) + identity_mask * diagonal_part[:, :, None]


def draw_coarse_x(key, part):
    return coarse_inverse(jax.random.fold_in(key, 1), CX)


def draw_coarse_y(key, part):
    return coarse_inverse(jax.random.fold_in(key, 2), TILE)


def draw_obstacle(key, part):
    key_first, key_second, key_radius = jax.random.split(jax.random.fold_in(key, 3), 3)
    centre_x = jax.random.randint(key_first, (TILES, 1, 1), TILE // 4, 3 * TILE // 4)
    centre_y = jax.random.randint(key_second, (TILES, 1, 1), TILE // 4, 3 * TILE // 4)
    radius = jax.random.randint(key_radius, (TILES, 1, 1), TILE // 8, TILE // 4 + 1)
    row_index = jnp.arange(TILE, dtype=jnp.int32)[None, :, None]
    col_index = jnp.arange(TILE, dtype=jnp.int32)[None, None, :]
    distance = (row_index - centre_x) ** 2 + (col_index - centre_y) ** 2
    return (distance <= radius * radius).astype(jnp.int32)


def draw_neighbors(key, part):
    block_count = TILES // TILES_DEV
    block_keys = jax.random.split(jax.random.fold_in(key, 4), block_count)
    within = jax.vmap(lambda block_key: jax.random.permutation(block_key, TILES_DEV))(block_keys).astype(jnp.int32)
    block_base = (jnp.arange(block_count, dtype=jnp.int32) * TILES_DEV)[:, None]
    ordering = (within + block_base).reshape(TILES).astype(jnp.int32)
    placing = jnp.zeros((TILES,), jnp.int32).at[ordering].set(jnp.arange(TILES, dtype=jnp.int32))
    grid_rows = TILES // TGY
    grid_x = placing // TGY
    grid_y = placing % TGY

    def lookup(target_x, target_y, usable):
        flat_place = jnp.clip(target_x * TGY + target_y, 0, TILES - 1)
        return jnp.where(usable, ordering[flat_place], TILES).astype(jnp.int32)
    west_tile = lookup(grid_x - 1, grid_y, grid_x > 0)
    east_tile = lookup(grid_x + 1, grid_y, grid_x < grid_rows - 1)
    south_tile = lookup(grid_x, grid_y - 1, grid_y > 0)
    north_tile = lookup(grid_x, grid_y + 1, grid_y < TGY - 1)
    return jnp.stack([west_tile, east_tile, south_tile, north_tile], axis=1)


def block_levels(rng, dims, shards, least, top_value):
    factor_of = 1.0
    for axis_at, shards_of in shards:
        heights = jax.random.uniform(jax.random.fold_in(jax.random.fold_in(rng, 6), axis_at), (shards_of,), jnp.float32, least / len(shards), top_value / len(shards))
        factor_of = factor_of * jnp.repeat(jnp.exp(heights), dims[axis_at] // shards_of).reshape((-1,) + (1,) * (len(dims) - 1 - axis_at))
    return factor_of


def noise(stream_key, dims, width, bound, cuts=(), kind=jnp.bfloat16):
    values = jax.random.normal(stream_key, dims, jnp.float32) * width
    if len(cuts) > 0:
        values = block_levels(stream_key, dims, cuts, -0.22, 0.18) * values
    return jnp.clip(values, min=-bound, max=bound).astype(kind)


def setup_inputs(seed: int = 0) -> dict:
    keys = jax.random.split(jax.random.key(seed), 9)
    starts = noise(keys[0], (SLICES, TILES, TILE, TILE), 1.0, 6.0, ((0, 16), (1, 8)), jnp.float32)
    diffusivity = jnp.clip(jnp.exp(math.log(0.2) - 1.609438 * jax.random.uniform(keys[1], (TILES, TILE, TILE), jnp.float32) ** block_levels(keys[1], (TILES, TILE, TILE), ((0, 8),), -0.2, 0.2)), 0.04, 0.2)
    velocity = jnp.clip(jax.random.uniform(keys[2], (2, TILES, TILE, TILE), jnp.float32, -0.1, 0.1) * block_levels(keys[2], (2, TILES, TILE, TILE), ((1, 8),), -0.4, 0.0), -0.1, 0.1)
    obstacle = draw_obstacle(jax.random.fold_in(keys[8], 71), 0)
    substep_scale = jnp.clip(jnp.exp(jax.random.uniform(keys[4], (SUB,), jnp.float32, math.log(0.5), math.log(1.0))), 0.5, 1.0)
    neighbors = draw_neighbors(jax.random.fold_in(keys[8], 71), 0)
    coarse_x = draw_coarse_x(jax.random.fold_in(keys[8], 71), 0)
    coarse_y = draw_coarse_y(jax.random.fold_in(keys[8], 71), 0)
    return dict(starts=starts, diffusivity=diffusivity, velocity=velocity, obstacle=obstacle, substep_scale=substep_scale, neighbors=neighbors, coarse_x=coarse_x, coarse_y=coarse_y)


exact_precision = lax.Precision.HIGHEST


def restrict(values):
    return 0.5 * (values[..., 0::2, :] + values[..., 1::2, :])


def prolong(coarse_values):
    return jnp.repeat(coarse_values, 2, axis=-2)


def apply_coarse(coarse_values, matrix_x, matrix_y):
    mixed_x = jnp.einsum("tij,...tjk->...tik", matrix_x, coarse_values, precision=exact_precision)
    return jnp.einsum("...tik,tlk->...til", mixed_x, matrix_y, precision=exact_precision)


def fine_propagate(start_state, diffusivity, speed_x, speed_y, open_cells, substep_scale, neighbors):
    def advance(current, strength):
        own_faces = jnp.stack([current[:, 0, :], current[:, -1, :], current[:, :, 0], current[:, :, -1]], axis=1)
        padded_faces = jnp.concatenate([own_faces, jnp.zeros_like(own_faces[:1])], axis=0)
        west_face = padded_faces[neighbors[:, 0], 1]
        east_face = padded_faces[neighbors[:, 1], 0]
        south_face = padded_faces[neighbors[:, 2], 3]
        north_face = padded_faces[neighbors[:, 3], 2]
        from_west = jnp.concatenate([west_face[:, None, :], current[:, :-1, :]], axis=1)
        from_east = jnp.concatenate([current[:, 1:, :], east_face[:, None, :]], axis=1)
        from_south = jnp.concatenate([south_face[:, :, None], current[:, :, :-1]], axis=2)
        from_north = jnp.concatenate([current[:, :, 1:], north_face[:, :, None]], axis=2)
        laplace = from_west + from_east + from_south + from_north - 4.0 * current
        transport = speed_x * (from_east - from_west) + speed_y * (from_north - from_south)
        updated = open_cells * (current + strength * diffusivity * laplace - 0.5 * transport)
        return updated, None

    final_state, unused = lax.scan(advance, start_state, substep_scale)
    return final_state


def reference(starts, diffusivity, velocity, obstacle, substep_scale, neighbors, coarse_x, coarse_y):
    open_cells = 1.0 - obstacle.astype(jnp.float32)
    fine_ends = lax.map(lambda start_state: fine_propagate(start_state, diffusivity, velocity[0], velocity[1], open_cells, substep_scale, neighbors), starts)
    correction = fine_ends - prolong(apply_coarse(restrict(starts), coarse_x, coarse_y))
    coarse_jump = restrict(correction)

    def sweep(state_now, jump):
        return apply_coarse(state_now, coarse_x, coarse_y) + jump, state_now

    last_state, coarse_states = lax.scan(sweep, restrict(starts[0]), coarse_jump)
    slice_ends = prolong(apply_coarse(coarse_states, coarse_x, coarse_y)) + correction
    next_starts = jnp.concatenate([starts[:1], slice_ends[:-1]], axis=0)
    return slice_ends, next_starts - starts
```

```python
import jax
import jax.numpy as jnp
from jax import lax
from jax.experimental import pallas as pl
from jax.experimental.pallas import tpu as pltpu
from jax.sharding import PartitionSpec as P

MESH = pl.DeviceIdType.MESH
SUB = 12
PLACES = 8
TILE = 128
CX = 64
SLICES = 16
BLOCK = 32
F32 = jnp.float32
BF16 = jnp.bfloat16


def halves(value):
    high = value.astype(BF16)
    return high, (value - high.astype(F32)).astype(BF16)


def product(left, right):
    left_high, left_low = left
    right_high, right_low = right
    total = jnp.dot(left_high, right_low, preferred_element_type=F32)
    total = total + jnp.dot(left_low, right_high, preferred_element_type=F32)
    return total + jnp.dot(left_high, right_high, preferred_element_type=F32)


def place_order(neighbors, space):
    first = jnp.int32(0)
    for t in range(PLACES):
        first = first + jnp.where(neighbors[t, 2] == PLACES * 8, t, 0)
    first = jnp.clip(first, 0, PLACES - 1)
    order = [first]
    for _ in range(PLACES - 1):
        order.append(jnp.clip(neighbors[order[-1], 3] - space * PLACES, 0, PLACES - 1))
    return order


def fine_kernel(
    scale, neighbors, starts_hbm, diff_hbm, vel_hbm, obst_hbm, cx_hbm, cy_hbm,
    sum_out, coarse_out, half_out, prev_out,
    starts, diff, vel, obst, cx, cy, load_sem,
    state, coef_d, coef_a, coef_b, west, east, west_past, east_past,
    xh, xl, yh, yl, coarse_starts, coarse_ends, mean, jump, half, half_prev,
    jumps, chain, coarse,
    halo_ss, halo_rs, jump_ss, jump_rs, half_ss, half_rs, chain_ss, chain_rs,
):
    tm = lax.axis_index("tm")
    space = lax.axis_index("space")
    core = lax.rem(tm, 2)
    chip = tm // 2
    is_owner = core == 0

    loads = [
        pltpu.make_async_copy(src, dst, load_sem.at[i])
        for i, (src, dst) in enumerate(
            [(starts_hbm, starts), (diff_hbm, diff), (obst_hbm, obst), (vel_hbm, vel),
             (cx_hbm, cx), (cy_hbm, cy)]
        )
    ]
    for load in loads:
        load.start()

    barrier = pltpu.get_barrier_semaphore()

    def greet(target_tm, target_space):
        pl.semaphore_signal(
            barrier, inc=1, device_id=(target_tm, target_space), device_id_type=MESH
        )

    @pl.when(space > 0)
    def _():
        greet(tm, space - 1)

    @pl.when(space < 7)
    def _():
        greet(tm, space + 1)

    def greet_slice(i, carry):
        greet(lax.rem(tm + i, SLICES), space)
        return carry

    lax.fori_loop(1, SLICES, greet_slice, 0)

    order = place_order(neighbors, space)

    for load in loads[:4]:
        load.wait()
    for p in range(PLACES):
        t = order[p]

        def convert(i, carry):
            rows = pl.ds(pl.multiple_of(i * 8, 8), 8)
            spread = pl.ds(i * 64 + p, 8, stride=8)
            open_cells = 1.0 - obst[t, rows, :].astype(F32)
            state[spread, :] = starts[t, rows, :]
            coef_d[spread, :] = open_cells * diff[t, rows, :]
            coef_a[spread, :] = (0.5 * open_cells) * vel[0, t, rows, :]
            coef_b[spread, :] = (0.5 * open_cells) * vel[1, t, rows, :]
            return carry

        lax.fori_loop(0, TILE // 8, convert, 0, unroll=4)

    def row(ref, r):
        at = r * 8 if isinstance(r, int) else pl.multiple_of(r * 8, 8)
        return ref[pl.ds(at, 8), :]

    state[pl.ds(TILE * 8, 8), :] = jnp.zeros((8, TILE), F32)
    for q, ref in enumerate((state, coef_d, coef_a, coef_b)):
        for i in range(SUB):
            west[q, SUB + i] = row(ref, i)
            east[q, i] = row(ref, TILE - SUB + i)

    @pl.when(space == 0)
    def _():
        west[:, 0:SUB] = jnp.zeros((4, SUB, 8, TILE), F32)

    @pl.when(space == 7)
    def _():
        east[:, SUB : 2 * SUB] = jnp.zeros((4, SUB, 8, TILE), F32)

    greeted = SLICES - 1 + jnp.where(space > 0, 1, 0) + jnp.where(space < 7, 1, 0)
    pl.semaphore_wait(barrier, greeted)

    to_west = pltpu.make_async_remote_copy(
        west.at[:, SUB : 2 * SUB], east.at[:, SUB : 2 * SUB], halo_ss.at[0], halo_rs.at[1],
        device_id=(tm, jnp.maximum(space - 1, 0)), device_id_type=MESH,
    )
    to_east = pltpu.make_async_remote_copy(
        east.at[:, 0:SUB], west.at[:, 0:SUB], halo_ss.at[1], halo_rs.at[0],
        device_id=(tm, jnp.minimum(space + 1, 7)), device_id_type=MESH,
    )

    @pl.when(space > 0)
    def _():
        to_west.start()

    @pl.when(space < 7)
    def _():
        to_east.start()

    lane = lax.broadcasted_iota(jnp.int32, (8, TILE), 1)
    sub = lax.broadcasted_iota(jnp.int32, (8, TILE), 0)
    south_face = lane == 0
    north_face = lane == TILE - 1
    south_end = jnp.logical_and(south_face, sub == 0)
    north_end = jnp.logical_and(north_face, sub == 7)

    def update(before, now, after, d, a, b, strength):
        south = pltpu.roll(now, 1, 1)
        south = jnp.where(south_face, pltpu.roll(south, 1, 0), south)
        south = jnp.where(south_end, 0.0, south)
        north = pltpu.roll(now, TILE - 1, 1)
        north = jnp.where(north_face, pltpu.roll(north, 7, 0), north)
        north = jnp.where(north_end, 0.0, north)
        laplace = (before + after) + (south + north) - 4.0 * now
        kept = jnp.where(d > 0.0, now, 0.0)
        return (
            kept + (strength * d) * laplace - a * (after - before) - b * (north - south)
        )

    for load in loads[4:]:
        load.wait()
    for p in range(PLACES):
        t = order[p]
        x_high, x_low = halves(cx[t])
        xh[p] = x_high
        xl[p] = x_low
        y_high, y_low = halves(cy[t].T)
        yh[p] = y_high
        yl[p] = y_low
        coarse_starts[p] = 0.5 * (
            starts[t, pl.ds(0, CX, stride=2), :] + starts[t, pl.ds(1, CX, stride=2), :]
        )

    def apply_coarse(p, values):
        mixed = product((xh[p], xl[p]), halves(values))
        return product(halves(mixed), (yh[p], yl[p]))

    for p in range(PLACES):
        coarse_ends[pl.ds(p * CX, CX), :] = apply_coarse(p, coarse_starts[p])

    def substep(s, carry):
        strength = scale[s]
        west_past[s, 0] = row(state, s)
        west_past[s, 1] = row(state, s + 1)
        east_past[s, 0] = row(state, TILE - 1 - s)
        east_past[s, 1] = row(state, TILE - 2 - s)

        def rows(i, before):
            base = i * BLOCK
            now = row(state, base)
            for r in range(BLOCK):
                at = base + r
                after = row(state, at + 1)
                fresh = update(
                    before, now, after, row(coef_d, at), row(coef_a, at), row(coef_b, at), strength
                )
                state[pl.ds(pl.multiple_of(at * 8, 8), 8), :] = fresh
                before, now = now, after
            return before

        lax.fori_loop(0, TILE // BLOCK, rows, jnp.zeros((8, TILE), F32))
        return carry

    lax.fori_loop(0, SUB, substep, 0)

    first_slice = jnp.where(tm == 0, 1.0, 0.0)

    def settle(i, even, odd):
        spread = pl.ds(i, 8, stride=CX)
        middle = 0.5 * (even + odd)
        coarse_end = coarse_ends[spread, :]
        mean[spread, :] = middle - coarse_end
        jump[spread, :] = middle - coarse_end + first_slice * coarse_end
        half[spread, :] = 0.5 * (even - odd)

    def settle_inner(i, carry):
        settle(i, row(state, 2 * i), row(state, 2 * i + 1))
        return carry

    lax.fori_loop(SUB // 2, CX - SUB // 2, settle_inner, 0, unroll=4)

    @pl.when(space > 0)
    def _():
        to_west.wait_send()
        to_east.wait_recv()

    @pl.when(space < 7)
    def _():
        to_east.wait_send()
        to_west.wait_recv()

    def border(s, carry):
        strength = scale[s]
        before = west[0, s]
        now = west[0, s + 1]
        for w in range(SUB):
            at = s + 1 + w
            after = west[0, at + 1] if w < SUB - 2 else west_past[s, w - (SUB - 2)]
            west[0, at] = update(
                before, now, after, west[1, at], west[2, at], west[3, at], strength
            )
            before, now = now, after
        after = east[0, 2 * SUB - 1 - s]
        now = east[0, 2 * SUB - 2 - s]
        for w in range(SUB):
            at = 2 * SUB - 2 - s - w
            before = east[0, at - 1] if w < SUB - 2 else east_past[s, w - (SUB - 2)]
            east[0, at] = update(
                before, now, after, east[1, at], east[2, at], east[3, at], strength
            )
            after, now = now, before
        return carry

    lax.fori_loop(0, SUB, border, 0)
    for i in range(SUB // 2):
        settle(i, west[0, SUB + 2 * i], west[0, SUB + 2 * i + 1])
        settle(CX - SUB // 2 + i, east[0, 2 * i], east[0, 2 * i + 1])

    def jump_copy(p):
        return pltpu.make_async_remote_copy(
            jump.at[pl.ds(p * CX, CX), :], jumps.at[tm], jump_ss.at[p], jump_rs.at[tm],
            device_id=(2 * p, space), device_id_type=MESH,
        )

    def jump_arrival(n):
        return pltpu.make_async_remote_copy(
            jump.at[pl.ds(0, CX), :], jumps.at[n], jump_ss.at[0], jump_rs.at[n],
            device_id=(tm, space), device_id_type=MESH,
        )

    for p in range(PLACES):
        @pl.when(jnp.logical_and(tm != 2 * p, tm < SLICES - 1))
        def _(p=p):
            jump_copy(p).start()

    half_copy = pltpu.make_async_remote_copy(
        half, half_prev, half_ss, half_rs,
        device_id=(jnp.minimum(tm + 1, SLICES - 1), space), device_id_type=MESH,
    )

    @pl.when(tm < SLICES - 1)
    def _():
        half_copy.start()

    def state_copy(n):
        return pltpu.make_async_remote_copy(
            chain.at[n], coarse.at[chip], chain_ss.at[n], chain_rs.at[chip],
            device_id=(n, space), device_id_type=MESH,
        )

    def state_arrival(p):
        return pltpu.make_async_remote_copy(
            chain.at[0], coarse.at[p], chain_ss.at[0], chain_rs.at[p],
            device_id=(tm, space), device_id_type=MESH,
        )

    @pl.when(is_owner)
    def _():
        jumps[tm] = jump[pl.ds(pl.multiple_of(chip * CX, CX), CX), :]

        def link(n, values):
            @pl.when(n != tm)
            def _():
                jump_arrival(n).wait_recv()

            values = jumps[n] + jnp.where(n > 0, 1.0, 0.0) * apply_coarse(chip, values)
            chain[n + 1] = values

            @pl.when(n + 1 != tm)
            def _():
                state_copy(n + 1).start()

            @pl.when(n + 1 == tm)
            def _():
                coarse[chip] = values

            return values

        lax.fori_loop(0, SLICES - 1, link, jnp.zeros((CX, TILE), F32))

    @pl.when(tm == 0)
    def _():
        coarse[...] = coarse_starts[...]

    half_out[...] = half[...]

    for p in range(PLACES):
        remote = jnp.logical_and(tm > 0, tm != 2 * p)

        @pl.when(remote)
        def _(p=p):
            state_arrival(p).wait_recv()

        values = coarse[p]
        coarse_out[pl.ds(p * CX, CX), :] = values
        sum_out[pl.ds(p * CX, CX), :] = apply_coarse(p, values) + mean[pl.ds(p * CX, CX), :]

    @pl.when(tm > 0)
    def _():
        half_copy.wait_recv()
        prev_out[...] = half_prev[...]

    @pl.when(tm == 0)
    def _():
        prev_out[...] = jnp.zeros_like(prev_out)

    for p in range(PLACES):
        @pl.when(jnp.logical_and(tm != 2 * p, tm < SLICES - 1))
        def _(p=p):
            jump_copy(p).wait_send()

    @pl.when(tm < SLICES - 1)
    def _():
        half_copy.wait_send()

    @pl.when(is_owner)
    def _():
        def sent(n, carry):
            @pl.when(n != tm)
            def _():
                state_copy(n).wait_send()

            return carry

        lax.fori_loop(1, SLICES, sent, 0)


def finish_kernel(neighbors, starts, sums, coarse, half, prev, ends_out, step_out):
    tm = lax.axis_index("tm")
    order = place_order(neighbors, lax.axis_index("space"))
    later = jnp.where(tm > 0, 1.0, 0.0)
    for p in range(PLACES):
        t = order[p]
        rows = pl.ds(p * CX, CX)
        even, odd = pl.ds(0, CX, stride=2), pl.ds(1, CX, stride=2)
        total, difference = sums[rows, :], half[rows, :]
        ends_out[t, even, :] = total + difference
        ends_out[t, odd, :] = total - difference
        total, difference = coarse[rows, :], prev[rows, :]
        step_out[t, even, :] = later * (total + difference - starts[t, even, :])
        step_out[t, odd, :] = later * (total - difference - starts[t, odd, :])


def on_device(
    starts, diffusivity, velocity, obstacle, substep_scale, neighbors, coarse_x, coarse_y
):
    smem = pl.BlockSpec(memory_space=pltpu.SMEM)
    vmem = pl.BlockSpec(memory_space=pltpu.VMEM)
    anywhere = pl.BlockSpec(memory_space=pl.ANY)
    tiles = (PLACES, TILE, TILE)
    places = jax.ShapeDtypeStruct((PLACES * CX, TILE), F32)
    dma = pltpu.SemaphoreType.DMA
    starts = starts[0]
    sums, coarse, half, prev = pl.pallas_call(
        fine_kernel,
        out_shape=(places,) * 4,
        in_specs=[smem, smem] + [anywhere] * 6,
        out_specs=(vmem,) * 4,
        scratch_shapes=[
            pltpu.VMEM(tiles, F32),
            pltpu.VMEM(tiles, F32),
            pltpu.VMEM((2,) + tiles, F32),
            pltpu.VMEM(tiles, jnp.int32),
            pltpu.VMEM((PLACES, CX, CX), F32),
            pltpu.VMEM(tiles, F32),
            dma((6,)),
            pltpu.VMEM((TILE * 8 + 8, TILE), F32),
            pltpu.VMEM((TILE * 8, TILE), F32),
            pltpu.VMEM((TILE * 8, TILE), F32),
            pltpu.VMEM((TILE * 8, TILE), F32),
            pltpu.VMEM((4, 2 * SUB, 8, TILE), F32),
            pltpu.VMEM((4, 2 * SUB, 8, TILE), F32),
            pltpu.VMEM((SUB, 2, 8, TILE), F32),
            pltpu.VMEM((SUB, 2, 8, TILE), F32),
            pltpu.VMEM((PLACES, CX, CX), BF16),
            pltpu.VMEM((PLACES, CX, CX), BF16),
            pltpu.VMEM(tiles, BF16),
            pltpu.VMEM(tiles, BF16),
            pltpu.VMEM((PLACES, CX, TILE), F32),
            pltpu.VMEM((PLACES * CX, TILE), F32),
            pltpu.VMEM((PLACES * CX, TILE), F32),
            pltpu.VMEM((PLACES * CX, TILE), F32),
            pltpu.VMEM((PLACES * CX, TILE), F32),
            pltpu.VMEM((PLACES * CX, TILE), F32),
            pltpu.VMEM((SLICES, CX, TILE), F32),
            pltpu.VMEM((SLICES, CX, TILE), F32),
            pltpu.VMEM((PLACES, CX, TILE), F32),
            dma((2,)),
            dma((2,)),
            dma((PLACES,)),
            dma((SLICES,)),
            dma,
            dma,
            dma((SLICES,)),
            dma((PLACES,)),
        ],
        compiler_params=pltpu.CompilerParams(
            collective_id=0, has_side_effects=True, vmem_limit_bytes=60 << 20
        ),
    )(substep_scale, neighbors, starts, diffusivity, velocity, obstacle, coarse_x, coarse_y)
    ends, step = pl.pallas_call(
        finish_kernel,
        out_shape=(jax.ShapeDtypeStruct(tiles, F32),) * 2,
        in_specs=[smem] + [vmem] * 5,
        out_specs=(vmem, vmem),
        compiler_params=pltpu.CompilerParams(vmem_limit_bytes=40 << 20),
    )(neighbors, starts, sums, coarse, half, prev)
    return ends[None], step[None]


def solution(mesh):
    placed = (
        P("tm", "space", None, None),
        P("space", None, None),
        P(None, "space", None, None),
        P("space", None, None),
        P(),
        P("space", None),
        P("space", None, None),
        P("space", None, None),
    )
    return jax.shard_map(
        on_device,
        mesh=mesh,
        in_specs=placed,
        out_specs=(P("tm", "space", None, None), P("tm", "space", None, None)),
        check_vma=False,
    )
```

```python
import jax
import jax.numpy as jnp
from jax import lax
from jax.experimental import pallas as pl
from jax.experimental.pallas import tpu as pltpu
from jax.sharding import PartitionSpec as P

MESH = pl.DeviceIdType.MESH
SUB = 12
PLACES = 8
TILE = 128
CX = 64
MID = 48
SLICES = 16
BLOCK = 32
F32 = jnp.float32
BF16 = jnp.bfloat16


def halves(value):
    high = value.astype(BF16)
    return high, (value - high.astype(F32)).astype(BF16)


def product(left, right):
    left_high, left_low = left
    right_high, right_low = right
    total = jnp.dot(left_high, right_low, preferred_element_type=F32)
    total = total + jnp.dot(left_low, right_high, preferred_element_type=F32)
    return total + jnp.dot(left_high, right_high, preferred_element_type=F32)


def place_order(neighbors, space):
    first = jnp.int32(0)
    for t in range(PLACES):
        first = first + jnp.where(neighbors[2, t] == PLACES * 8, t, 0)
    first = jnp.clip(first, 0, PLACES - 1)
    order = [first]
    for _ in range(PLACES - 1):
        order.append(jnp.clip(neighbors[3, order[-1]] - space * PLACES, 0, PLACES - 1))
    return order


def fine_kernel(
    scale, neighbors, starts_hbm, diff_hbm, vel_hbm, obst_hbm, cx_hbm, cy_hbm,
    sum_out, coarse_out, half_out, prev_out,
    starts, diff, vel, obst, cx, cy, load_sem,
    state, coef_d, coef_a, coef_b, west, east, west_past, east_past,
    xh, xl, yh, yl, coarse_starts, coarse_ends, mean, half,
    jump_mid, jump_edge, half_mid, half_edge, prev_mid, prev_edge, jumps_mid, jumps_edge,
    chain, coarse,
    halo_ss, halo_rs, jump_ss, jump_rs, half_ss, half_rs, chain_ss, chain_rs,
):
    tm = lax.axis_index("tm")
    space = lax.axis_index("space")
    core = lax.rem(tm, 2)
    chip = tm // 2
    is_owner = core == 0

    loads = [
        pltpu.make_async_copy(src, dst, load_sem.at[i])
        for i, (src, dst) in enumerate(
            [(starts_hbm, starts), (diff_hbm, diff), (obst_hbm, obst), (vel_hbm, vel),
             (cx_hbm, cx), (cy_hbm, cy)]
        )
    ]
    for load in loads:
        load.start()

    barrier = pltpu.get_barrier_semaphore()

    def greet(target_tm, target_space):
        pl.semaphore_signal(
            barrier, inc=1, device_id=(target_tm, target_space), device_id_type=MESH
        )

    @pl.when(space > 0)
    def _():
        greet(tm, space - 1)

    @pl.when(space < 7)
    def _():
        greet(tm, space + 1)

    def greet_slice(i, carry):
        greet(lax.rem(tm + i, SLICES), space)
        return carry

    lax.fori_loop(1, SLICES, greet_slice, 0)

    order = place_order(neighbors, space)

    for load in loads[:4]:
        load.wait()
    for p in range(PLACES):
        t = order[p]

        def convert(i, carry):
            rows = pl.ds(pl.multiple_of(i * 8, 8), 8)
            spread = pl.ds(i * 64 + p, 8, stride=8)
            open_cells = 1.0 - obst[t, rows, :].astype(F32)
            state[spread, :] = starts[t, rows, :]
            coef_d[spread, :] = open_cells * diff[t, rows, :]
            coef_a[spread, :] = (0.5 * open_cells) * vel[0, t, rows, :]
            coef_b[spread, :] = (0.5 * open_cells) * vel[1, t, rows, :]
            return carry

        lax.fori_loop(0, TILE // 8, convert, 0, unroll=4)

    def row(ref, r):
        at = r * 8 if isinstance(r, int) else pl.multiple_of(r * 8, 8)
        return ref[pl.ds(at, 8), :]

    state[pl.ds(TILE * 8, 8), :] = jnp.zeros((8, TILE), F32)
    for q, ref in enumerate((state, coef_d, coef_a, coef_b)):
        for i in range(SUB):
            west[q, SUB + i] = row(ref, i)
            east[q, i] = row(ref, TILE - SUB + i)

    @pl.when(space == 0)
    def _():
        west[:, 0:SUB] = jnp.zeros((4, SUB, 8, TILE), F32)

    @pl.when(space == 7)
    def _():
        east[:, SUB : 2 * SUB] = jnp.zeros((4, SUB, 8, TILE), F32)

    greeted = SLICES - 1 + jnp.where(space > 0, 1, 0) + jnp.where(space < 7, 1, 0)
    pl.semaphore_wait(barrier, greeted)

    to_west = pltpu.make_async_remote_copy(
        west.at[:, SUB : 2 * SUB], east.at[:, SUB : 2 * SUB], halo_ss.at[0], halo_rs.at[1],
        device_id=(tm, jnp.maximum(space - 1, 0)), device_id_type=MESH,
    )
    to_east = pltpu.make_async_remote_copy(
        east.at[:, 0:SUB], west.at[:, 0:SUB], halo_ss.at[1], halo_rs.at[0],
        device_id=(tm, jnp.minimum(space + 1, 7)), device_id_type=MESH,
    )

    @pl.when(space > 0)
    def _():
        to_west.start()

    @pl.when(space < 7)
    def _():
        to_east.start()

    lane = lax.broadcasted_iota(jnp.int32, (8, TILE), 1)
    sub = lax.broadcasted_iota(jnp.int32, (8, TILE), 0)
    south_face = lane == 0
    north_face = lane == TILE - 1
    south_end = jnp.logical_and(south_face, sub == 0)
    north_end = jnp.logical_and(north_face, sub == 7)

    def update(before, now, after, d, a, b, strength):
        south = pltpu.roll(now, 1, 1)
        south = jnp.where(south_face, pltpu.roll(south, 1, 0), south)
        south = jnp.where(south_end, 0.0, south)
        north = pltpu.roll(now, TILE - 1, 1)
        north = jnp.where(north_face, pltpu.roll(north, 7, 0), north)
        north = jnp.where(north_end, 0.0, north)
        laplace = (before + after) + (south + north) - 4.0 * now
        kept = jnp.where(d > 0.0, now, 0.0)
        return (
            kept + (strength * d) * laplace - a * (after - before) - b * (north - south)
        )

    for load in loads[4:]:
        load.wait()
    for p in range(PLACES):
        t = order[p]
        x_high, x_low = halves(cx[t])
        xh[p] = x_high
        xl[p] = x_low
        y_high, y_low = halves(cy[t].T)
        yh[p] = y_high
        yl[p] = y_low
        coarse_starts[p] = 0.5 * (
            starts[t, pl.ds(0, CX, stride=2), :] + starts[t, pl.ds(1, CX, stride=2), :]
        )

    def apply_coarse(p, values):
        mixed = product((xh[p], xl[p]), halves(values))
        return product(halves(mixed), (yh[p], yl[p]))

    for p in range(PLACES):
        coarse_ends[pl.ds(p * CX, CX), :] = apply_coarse(p, coarse_starts[p])

    def substep(s, carry):
        strength = scale[s]
        west_past[s, 0] = row(state, s)
        west_past[s, 1] = row(state, s + 1)
        east_past[s, 0] = row(state, TILE - 1 - s)
        east_past[s, 1] = row(state, TILE - 2 - s)

        def rows(i, before):
            base = i * BLOCK
            now = row(state, base)
            for r in range(BLOCK):
                at = base + r
                after = row(state, at + 1)
                fresh = update(
                    before, now, after, row(coef_d, at), row(coef_a, at), row(coef_b, at), strength
                )
                state[pl.ds(pl.multiple_of(at * 8, 8), 8), :] = fresh
                before, now = now, after
            return before

        lax.fori_loop(0, TILE // BLOCK, rows, jnp.zeros((8, TILE), F32))
        return carry

    lax.fori_loop(0, SUB, substep, 0)

    first_slice = jnp.where(tm == 0, 1.0, 0.0)

    def settle(i, even, odd):
        spread = pl.ds(i, 8, stride=CX)
        middle = 0.5 * (even + odd)
        coarse_end = coarse_ends[spread, :]
        mean[spread, :] = middle - coarse_end
        half[spread, :] = 0.5 * (even - odd)

    def settle_inner(i, carry):
        settle(i, row(state, 2 * i), row(state, 2 * i + 1))
        return carry

    lax.fori_loop(SUB // 2, CX - SUB // 2, settle_inner, 0, unroll=4)

    jump_parts = ((jump_mid, jumps_mid), (jump_edge, jumps_edge))

    def jump_copy(p, i):
        source, target = jump_parts[i]
        return pltpu.make_async_remote_copy(
            source.at[p], target.at[tm], jump_ss.at[i, p], jump_rs.at[i, tm],
            device_id=(2 * p, space), device_id_type=MESH,
        )

    def jump_arrival(n, i):
        source, target = jump_parts[i]
        return pltpu.make_async_remote_copy(
            source.at[0], target.at[n], jump_ss.at[i, 0], jump_rs.at[i, n],
            device_id=(tm, space), device_id_type=MESH,
        )

    half_copies = [
        pltpu.make_async_remote_copy(
            source, target, half_ss.at[i], half_rs.at[i],
            device_id=(jnp.minimum(tm + 1, SLICES - 1), space), device_id_type=MESH,
        )
        for i, (source, target) in enumerate(((half_mid, prev_mid), (half_edge, prev_edge)))
    ]
    passes_on = tm < SLICES - 1

    def sends_to(p):
        return jnp.logical_and(tm != 2 * p, passes_on)

    for p in range(PLACES):
        inner = pl.ds(p * CX + 8, MID)
        jump_mid[p] = mean[inner, :] + first_slice * coarse_ends[inner, :]

        @pl.when(sends_to(p))
        def _(p=p):
            jump_copy(p, 0).start()

    for p in range(PLACES):
        half_mid[p] = half[pl.ds(p * CX + 8, MID), :]

    @pl.when(passes_on)
    def _():
        half_copies[0].start()

    @pl.when(space > 0)
    def _():
        to_west.wait_send()
        to_east.wait_recv()

    @pl.when(space < 7)
    def _():
        to_east.wait_send()
        to_west.wait_recv()

    def border(s, carry):
        strength = scale[s]
        low, high = carry[:SUB], carry[SUB:]
        low = low + (west_past[s, 0], west_past[s, 1])
        high = high + (east_past[s, 0], east_past[s, 1])
        fresh_low, fresh_high = [], []
        for w in range(SUB):
            at = s + 1 + w
            fresh_low.append(
                update(
                    low[w], low[w + 1], low[w + 2],
                    west[1, at], west[2, at], west[3, at], strength,
                )
            )
            at = 2 * SUB - 2 - s - w
            fresh_high.append(
                update(
                    high[w + 2], high[w + 1], high[w],
                    east[1, at], east[2, at], east[3, at], strength,
                )
            )
        return tuple(fresh_low) + tuple(fresh_high)

    edge_rows = lax.fori_loop(
        0, SUB, border,
        tuple(west[0, w] for w in range(SUB))
        + tuple(east[0, 2 * SUB - 1 - w] for w in range(SUB)),
    )
    low, high = edge_rows[:SUB], edge_rows[SUB:][::-1]
    for i in range(SUB // 2):
        settle(i, low[2 * i], low[2 * i + 1])
        settle(CX - SUB // 2 + i, high[2 * i], high[2 * i + 1])

    for p in range(PLACES):
        for at, first in ((0, 0), (8, CX - 8)):
            rows = pl.ds(p * CX + first, 8)
            jump_edge[p, at : at + 8] = mean[rows, :] + first_slice * coarse_ends[rows, :]

        @pl.when(sends_to(p))
        def _(p=p):
            jump_copy(p, 1).start()

    for p in range(PLACES):
        half_edge[p, 0:8] = half[pl.ds(p * CX, 8), :]
        half_edge[p, 8:16] = half[pl.ds(p * CX + CX - 8, 8), :]

    @pl.when(passes_on)
    def _():
        half_copies[1].start()

    def state_copy(n):
        return pltpu.make_async_remote_copy(
            chain.at[n], coarse.at[chip], chain_ss.at[n], chain_rs.at[chip],
            device_id=(n, space), device_id_type=MESH,
        )

    def state_arrival(p):
        return pltpu.make_async_remote_copy(
            chain.at[0], coarse.at[p], chain_ss.at[0], chain_rs.at[p],
            device_id=(tm, space), device_id_type=MESH,
        )

    @pl.when(is_owner)
    def _():
        jumps_mid[tm] = jump_mid[chip]
        jumps_edge[tm] = jump_edge[chip]

        def link(n, values):
            @pl.when(n != tm)
            def _():
                for i in range(2):
                    jump_arrival(n, i).wait_recv()

            own = jnp.concatenate(
                [jumps_edge[n, 0:8], jumps_mid[n], jumps_edge[n, 8:16]], axis=0
            )
            values = own + jnp.where(n > 0, 1.0, 0.0) * apply_coarse(chip, values)
            chain[n + 1] = values

            @pl.when(n + 1 != tm)
            def _():
                state_copy(n + 1).start()

            @pl.when(n + 1 == tm)
            def _():
                coarse[chip] = values

            return values

        lax.fori_loop(0, SLICES - 1, link, jnp.zeros((CX, TILE), F32))

    @pl.when(tm == 0)
    def _():
        coarse[...] = coarse_starts[...]

    half_out[...] = half[...]

    for p in range(PLACES):
        remote = jnp.logical_and(tm > 0, tm != 2 * p)

        @pl.when(remote)
        def _(p=p):
            state_arrival(p).wait_recv()

        values = coarse[p]
        coarse_out[pl.ds(p * CX, CX), :] = values
        sum_out[pl.ds(p * CX, CX), :] = apply_coarse(p, values) + mean[pl.ds(p * CX, CX), :]

    @pl.when(tm > 0)
    def _():
        for copy in half_copies:
            copy.wait_recv()
        for p in range(PLACES):
            prev_out[pl.ds(p * CX, 8), :] = prev_edge[p, 0:8]
            prev_out[pl.ds(p * CX + 8, MID), :] = prev_mid[p]
            prev_out[pl.ds(p * CX + CX - 8, 8), :] = prev_edge[p, 8:16]

    @pl.when(tm == 0)
    def _():
        prev_out[...] = jnp.zeros_like(prev_out)

    for p in range(PLACES):
        @pl.when(sends_to(p))
        def _(p=p):
            for i in range(2):
                jump_copy(p, i).wait_send()

    @pl.when(passes_on)
    def _():
        for copy in half_copies:
            copy.wait_send()

    @pl.when(is_owner)
    def _():
        def sent(n, carry):
            @pl.when(n != tm)
            def _():
                state_copy(n).wait_send()

            return carry

        lax.fori_loop(1, SLICES, sent, 0)


def finish_kernel(
    neighbors, starts_hbm, sums_hbm, coarse_hbm, half_hbm, prev_hbm, ends_hbm, step_hbm,
    starts, sums, coarse, half, prev, ends, step, load_sem, store_sem,
):
    loads = [
        pltpu.make_async_copy(src, dst, load_sem.at[i])
        for i, (src, dst) in enumerate(
            [(sums_hbm, sums), (half_hbm, half), (coarse_hbm, coarse), (prev_hbm, prev),
             (starts_hbm, starts)]
        )
    ]
    for load in loads:
        load.start()
    tm = lax.axis_index("tm")
    order = place_order(neighbors, lax.axis_index("space"))
    later = jnp.where(tm > 0, 1.0, 0.0)
    even, odd = pl.ds(0, CX, stride=2), pl.ds(1, CX, stride=2)
    loads[0].wait()
    loads[1].wait()
    stores = []
    for p in range(PLACES):
        t = order[p]
        rows = pl.ds(p * CX, CX)
        total, difference = sums[rows, :], half[rows, :]
        ends[p, even, :] = total + difference
        ends[p, odd, :] = total - difference
        stores.append(pltpu.make_async_copy(ends.at[p], ends_hbm.at[t], store_sem.at[0, p]))
        stores[-1].start()
    for load in loads[2:]:
        load.wait()
    for p in range(PLACES):
        t = order[p]
        rows = pl.ds(p * CX, CX)
        total, difference = coarse[rows, :], prev[rows, :]
        step[p, even, :] = later * (total + difference - starts[t, even, :])
        step[p, odd, :] = later * (total - difference - starts[t, odd, :])
        stores.append(pltpu.make_async_copy(step.at[p], step_hbm.at[t], store_sem.at[1, p]))
        stores[-1].start()
    for store in stores:
        store.wait()


def on_device(
    starts, diffusivity, velocity, obstacle, substep_scale, neighbors, coarse_x, coarse_y
):
    smem = pl.BlockSpec(memory_space=pltpu.SMEM)
    vmem = pl.BlockSpec(memory_space=pltpu.VMEM)
    anywhere = pl.BlockSpec(memory_space=pl.ANY)
    tiles = (PLACES, TILE, TILE)
    places = jax.ShapeDtypeStruct((PLACES * CX, TILE), F32)
    dma = pltpu.SemaphoreType.DMA
    starts = starts[0]
    neighbors = neighbors.T
    sums, coarse, half, prev = pl.pallas_call(
        fine_kernel,
        out_shape=(places,) * 4,
        in_specs=[smem, smem] + [anywhere] * 6,
        out_specs=(vmem,) * 4,
        scratch_shapes=[
            pltpu.VMEM(tiles, F32),
            pltpu.VMEM(tiles, F32),
            pltpu.VMEM((2,) + tiles, F32),
            pltpu.VMEM(tiles, jnp.int32),
            pltpu.VMEM((PLACES, CX, CX), F32),
            pltpu.VMEM(tiles, F32),
            dma((6,)),
            pltpu.VMEM((TILE * 8 + 8, TILE), F32),
            pltpu.VMEM((TILE * 8, TILE), F32),
            pltpu.VMEM((TILE * 8, TILE), F32),
            pltpu.VMEM((TILE * 8, TILE), F32),
            pltpu.VMEM((4, 2 * SUB, 8, TILE), F32),
            pltpu.VMEM((4, 2 * SUB, 8, TILE), F32),
            pltpu.VMEM((SUB, 2, 8, TILE), F32),
            pltpu.VMEM((SUB, 2, 8, TILE), F32),
            pltpu.VMEM((PLACES, CX, CX), BF16),
            pltpu.VMEM((PLACES, CX, CX), BF16),
            pltpu.VMEM(tiles, BF16),
            pltpu.VMEM(tiles, BF16),
            pltpu.VMEM((PLACES, CX, TILE), F32),
            pltpu.VMEM((PLACES * CX, TILE), F32),
            pltpu.VMEM((PLACES * CX, TILE), F32),
            pltpu.VMEM((PLACES * CX, TILE), F32),
            pltpu.VMEM((PLACES, MID, TILE), F32),
            pltpu.VMEM((PLACES, 16, TILE), F32),
            pltpu.VMEM((PLACES, MID, TILE), F32),
            pltpu.VMEM((PLACES, 16, TILE), F32),
            pltpu.VMEM((PLACES, MID, TILE), F32),
            pltpu.VMEM((PLACES, 16, TILE), F32),
            pltpu.VMEM((SLICES, MID, TILE), F32),
            pltpu.VMEM((SLICES, 16, TILE), F32),
            pltpu.VMEM((SLICES, CX, TILE), F32),
            pltpu.VMEM((PLACES, CX, TILE), F32),
            dma((2,)),
            dma((2,)),
            dma((2, PLACES)),
            dma((2, SLICES)),
            dma((2,)),
            dma((2,)),
            dma((SLICES,)),
            dma((PLACES,)),
        ],
        compiler_params=pltpu.CompilerParams(
            collective_id=0, has_side_effects=True, vmem_limit_bytes=60 << 20
        ),
    )(substep_scale, neighbors, starts, diffusivity, velocity, obstacle, coarse_x, coarse_y)
    ends, step = pl.pallas_call(
        finish_kernel,
        out_shape=(jax.ShapeDtypeStruct(tiles, F32),) * 2,
        in_specs=[smem] + [anywhere] * 5,
        out_specs=(anywhere, anywhere),
        scratch_shapes=[pltpu.VMEM(tiles, F32)]
        + [pltpu.VMEM((PLACES * CX, TILE), F32)] * 4
        + [pltpu.VMEM(tiles, F32)] * 2
        + [dma((5,)), dma((2, PLACES))],
        compiler_params=pltpu.CompilerParams(vmem_limit_bytes=60 << 20),
    )(neighbors, starts, sums, coarse, half, prev)
    return ends[None], step[None]


def solution(mesh):
    placed = (
        P("tm", "space", None, None),
        P("space", None, None),
        P(None, "space", None, None),
        P("space", None, None),
        P(),
        P("space", None),
        P("space", None, None),
        P("space", None, None),
    )
    return jax.shard_map(
        on_device,
        mesh=mesh,
        in_specs=placed,
        out_specs=(P("tm", "space", None, None), P("tm", "space", None, None)),
        check_vma=False,
    )
```

```python
import jax
import jax.numpy as jnp
from jax import lax
from jax.experimental import pallas as pl
from jax.experimental.pallas import tpu as pltpu
from jax.sharding import PartitionSpec as P

MESH = pl.DeviceIdType.MESH
SUB = 12
PLACES = 8
TILE = 128
CX = 64
MID = 48
SLICES = 16
F32 = jnp.float32
BF16 = jnp.bfloat16


def halves(value):
    high = value.astype(BF16)
    return high, (value - high.astype(F32)).astype(BF16)


def product(left, right):
    left_high, left_low = left
    right_high, right_low = right
    total = jnp.dot(left_high, right_low, preferred_element_type=F32)
    total = total + jnp.dot(left_low, right_high, preferred_element_type=F32)
    return total + jnp.dot(left_high, right_high, preferred_element_type=F32)


def place_order(neighbors, space):
    first = jnp.int32(0)
    for t in range(PLACES):
        first = first + jnp.where(neighbors[2, t] == PLACES * 8, t, 0)
    first = jnp.clip(first, 0, PLACES - 1)
    order = [first]
    for _ in range(PLACES - 1):
        order.append(jnp.clip(neighbors[3, order[-1]] - space * PLACES, 0, PLACES - 1))
    return order


def fine_kernel(
    scale_hbm, neighbors_hbm, starts_hbm, diff_hbm, vel_hbm, obst_hbm, cx_hbm, cy_hbm,
    sum_out, coarse_out, half_out, prev_out,
    scale, neighbors, starts_edge, diff_edge, vel_edge, obst_edge, starts, diff, vel, obst,
    cx, cy, load_sem, store_sem,
    state, coef_d, coef_a, coef_b, west, east, west_past, east_past,
    xh, xl, yh, yl, coarse_starts, coarse_ends, mean, half,
    jump_mid, jump_edge, half_mid, half_edge, prev_mid, prev_edge, jumps_mid, jumps_edge,
    chain, coarse, sums,
    halo_ss, halo_rs, jump_ss, jump_rs, half_ss, half_rs, chain_ss, chain_rs,
):
    tm = lax.axis_index("tm")
    space = lax.axis_index("space")
    core = lax.rem(tm, 2)
    chip = tm // 2
    is_owner = core == 0

    fields = (starts_hbm, diff_hbm, obst_hbm, vel_hbm)
    edges = (starts_edge, diff_edge, obst_edge, vel_edge)
    inner = (starts, diff, obst, vel)
    pairs = [(neighbors_hbm, neighbors), (scale_hbm, scale)]
    for first, at in ((0, 0), (TILE - 16, 16)):
        pairs += [
            (src.at[..., pl.ds(first, 16), :], dst.at[..., pl.ds(at, 16), :])
            for src, dst in zip(fields, edges)
        ]
    pairs += [
        (src.at[..., pl.ds(16, TILE - 32), :], dst) for src, dst in zip(fields, inner)
    ]
    pairs += [(cx_hbm, cx), (cy_hbm, cy)]
    loads = [
        pltpu.make_async_copy(src, dst, load_sem.at[i]) for i, (src, dst) in enumerate(pairs)
    ]
    for load in loads:
        load.start()

    barrier = pltpu.get_barrier_semaphore()

    def greet(target_tm, target_space):
        pl.semaphore_signal(
            barrier, inc=1, device_id=(target_tm, target_space), device_id_type=MESH
        )

    @pl.when(space > 0)
    def _():
        greet(tm, space - 1)

    @pl.when(space < 7)
    def _():
        greet(tm, space + 1)

    def greet_slice(i, carry):
        greet(lax.rem(tm + i, SLICES), space)
        return carry

    lax.fori_loop(1, SLICES, greet_slice, 0)

    def convert(p, block, at, sources):
        first, diffusion, tubes, speed = sources
        rows = pl.ds(at if isinstance(at, int) else pl.multiple_of(at, 8), 8)
        spread = pl.ds(block * 64 + p, 8, stride=8)
        t = order[p]
        open_cells = 1.0 - tubes[t, rows, :].astype(F32)
        state[spread, :] = first[t, rows, :]
        coef_d[spread, :] = open_cells * diffusion[t, rows, :]
        coef_a[spread, :] = (0.5 * open_cells) * speed[0, t, rows, :]
        coef_b[spread, :] = (0.5 * open_cells) * speed[1, t, rows, :]

    for load in loads[:10]:
        load.wait()
    order = place_order(neighbors, space)
    for p in range(PLACES):
        for i, block in enumerate((0, 1, TILE // 8 - 2, TILE // 8 - 1)):
            convert(p, block, 8 * i, edges)

    def row(ref, r):
        at = r * 8 if isinstance(r, int) else pl.multiple_of(r * 8, 8)
        return ref[pl.ds(at, 8), :]

    for q, ref in enumerate((state, coef_d, coef_a, coef_b)):
        for i in range(SUB):
            west[q, SUB + i] = row(ref, i)
            east[q, i] = row(ref, TILE - SUB + i)

    @pl.when(space == 0)
    def _():
        west[:, 0:SUB] = jnp.zeros((4, SUB, 8, TILE), F32)

    @pl.when(space == 7)
    def _():
        east[:, SUB : 2 * SUB] = jnp.zeros((4, SUB, 8, TILE), F32)

    greeted = SLICES - 1 + jnp.where(space > 0, 1, 0) + jnp.where(space < 7, 1, 0)

    to_west = pltpu.make_async_remote_copy(
        west.at[:, SUB : 2 * SUB], east.at[:, SUB : 2 * SUB], halo_ss.at[0], halo_rs.at[1],
        device_id=(tm, jnp.maximum(space - 1, 0)), device_id_type=MESH,
    )
    to_east = pltpu.make_async_remote_copy(
        east.at[:, 0:SUB], west.at[:, 0:SUB], halo_ss.at[1], halo_rs.at[0],
        device_id=(tm, jnp.minimum(space + 1, 7)), device_id_type=MESH,
    )

    lane = lax.broadcasted_iota(jnp.int32, (8, TILE), 1)
    sub = lax.broadcasted_iota(jnp.int32, (8, TILE), 0)
    south_face = lane == 0
    north_face = lane == TILE - 1
    north_wrap = jnp.logical_and(north_face, sub == 0)
    south_wrap = jnp.logical_and(south_face, sub == 7)

    def update(before, now, after, d, a, b, strength):
        south = jnp.where(north_face, pltpu.roll(now, 1, 0), now)
        south = pltpu.roll(jnp.where(north_wrap, 0.0, south), 1, 1)
        north = jnp.where(south_face, pltpu.roll(now, 7, 0), now)
        north = pltpu.roll(jnp.where(south_wrap, 0.0, north), TILE - 1, 1)
        laplace = (before + after) + (south + north) - 4.0 * now
        return now + (strength * d) * laplace - a * (after - before) - b * (north - south)

    pl.semaphore_wait(barrier, greeted)

    @pl.when(space > 0)
    def _():
        to_west.start()

    @pl.when(space < 7)
    def _():
        to_east.start()

    for load in loads[10:]:
        load.wait()
    state[pl.ds(TILE * 8, 8), :] = jnp.zeros((8, TILE), F32)
    for p in range(PLACES):

        def convert_inner(i, carry, p=p):
            convert(p, i + 2, i * 8, inner)
            return carry

        lax.fori_loop(0, TILE // 8 - 4, convert_inner, 0, unroll=4)

    for p in range(PLACES):
        t = order[p]
        x_high, x_low = halves(cx[t])
        xh[p] = x_high
        xl[p] = x_low
        y_high, y_low = halves(cy[t].T)
        yh[p] = y_high
        yl[p] = y_low
        for ref, at, target in (
            (starts_edge, 0, slice(0, 8)),
            (starts_edge, 16, slice(CX - 8, CX)),
            (starts, 0, slice(8, CX - 8)),
        ):
            count = target.stop - target.start
            coarse_starts[p, target] = 0.5 * (
                ref[t, pl.ds(at, count, stride=2), :] + ref[t, pl.ds(at + 1, count, stride=2), :]
            )

    def apply_coarse(p, values):
        mixed = product((xh[p], xl[p]), halves(values))
        return product(halves(mixed), (yh[p], yl[p]))

    for p in range(PLACES):
        coarse_ends[pl.ds(p * CX, CX), :] = apply_coarse(p, coarse_starts[p])

    def substep(s, carry):
        strength = scale[s]
        west_past[s, 0] = row(state, s)
        west_past[s, 1] = row(state, s + 1)
        east_past[s, 0] = row(state, TILE - 1 - s)
        east_past[s, 1] = row(state, TILE - 2 - s)
        before = jnp.zeros((8, TILE), F32)
        now = row(state, 0)
        for r in range(TILE):
            after = row(state, r + 1)
            state[r * 8 : r * 8 + 8, :] = update(
                before, now, after, row(coef_d, r), row(coef_a, r), row(coef_b, r), strength
            )
            before, now = now, after

        @pl.when(s == 0)
        def _():
            for r in range(TILE):
                here = slice(r * 8, r * 8 + 8)
                state[here, :] = jnp.where(coef_d[here, :] > 0.0, state[here, :], 0.0)

        return carry

    lax.fori_loop(0, SUB, substep, 0)

    first_slice = jnp.where(tm == 0, 1.0, 0.0)

    def settle(i, even, odd):
        spread = pl.ds(i, 8, stride=CX)
        middle = 0.5 * (even + odd)
        coarse_end = coarse_ends[spread, :]
        mean[spread, :] = middle - coarse_end
        half[spread, :] = 0.5 * (even - odd)

    def settle_inner(i, carry):
        settle(i, row(state, 2 * i), row(state, 2 * i + 1))
        return carry

    lax.fori_loop(SUB // 2, CX - SUB // 2, settle_inner, 0, unroll=4)

    jump_parts = ((jump_mid, jumps_mid), (jump_edge, jumps_edge))

    def jump_copy(p, i):
        source, target = jump_parts[i]
        return pltpu.make_async_remote_copy(
            source.at[p], target.at[tm], jump_ss.at[i, p], jump_rs.at[i, tm],
            device_id=(2 * p, space), device_id_type=MESH,
        )

    def jump_arrival(n, i):
        source, target = jump_parts[i]
        return pltpu.make_async_remote_copy(
            source.at[0], target.at[n], jump_ss.at[i, 0], jump_rs.at[i, n],
            device_id=(tm, space), device_id_type=MESH,
        )

    half_copies = [
        pltpu.make_async_remote_copy(
            source, target, half_ss.at[i], half_rs.at[i],
            device_id=(jnp.minimum(tm + 1, SLICES - 1), space), device_id_type=MESH,
        )
        for i, (source, target) in enumerate(((half_mid, prev_mid), (half_edge, prev_edge)))
    ]
    passes_on = tm < SLICES - 1

    def sends_to(p):
        return jnp.logical_and(tm != 2 * p, passes_on)

    for p in range(PLACES):
        rows = pl.ds(p * CX + 8, MID)
        jump_mid[p] = mean[rows, :] + first_slice * coarse_ends[rows, :]

        @pl.when(sends_to(p))
        def _(p=p):
            jump_copy(p, 0).start()

    for p in range(PLACES):
        half_mid[p] = half[pl.ds(p * CX + 8, MID), :]

    @pl.when(passes_on)
    def _():
        half_copies[0].start()

    @pl.when(space > 0)
    def _():
        to_west.wait_send()
        to_east.wait_recv()

    @pl.when(space < 7)
    def _():
        to_east.wait_send()
        to_west.wait_recv()

    def border(s, carry):
        strength = scale[s]
        low, high = carry[:SUB], carry[SUB:]
        low = low + (west_past[s, 0], west_past[s, 1])
        high = high + (east_past[s, 0], east_past[s, 1])
        fresh_low, fresh_high = [], []
        for w in range(SUB):
            at = s + 1 + w
            fresh = update(
                low[w], low[w + 1], low[w + 2], west[1, at], west[2, at], west[3, at], strength
            )
            fresh_low.append(jnp.where(west[1, at] > 0.0, fresh, 0.0))
            at = 2 * SUB - 2 - s - w
            fresh = update(
                high[w + 2], high[w + 1], high[w], east[1, at], east[2, at], east[3, at], strength
            )
            fresh_high.append(jnp.where(east[1, at] > 0.0, fresh, 0.0))
        return tuple(fresh_low) + tuple(fresh_high)

    edge_rows = lax.fori_loop(
        0, SUB, border,
        tuple(west[0, w] for w in range(SUB))
        + tuple(east[0, 2 * SUB - 1 - w] for w in range(SUB)),
    )
    low, high = edge_rows[:SUB], edge_rows[SUB:][::-1]
    for i in range(SUB // 2):
        settle(i, low[2 * i], low[2 * i + 1])
        settle(CX - SUB // 2 + i, high[2 * i], high[2 * i + 1])

    for p in range(PLACES):
        for at, first in ((0, 0), (8, CX - 8)):
            rows = pl.ds(p * CX + first, 8)
            jump_edge[p, at : at + 8] = mean[rows, :] + first_slice * coarse_ends[rows, :]

        @pl.when(sends_to(p))
        def _(p=p):
            jump_copy(p, 1).start()

    for p in range(PLACES):
        half_edge[p, 0:8] = half[pl.ds(p * CX, 8), :]
        half_edge[p, 8:16] = half[pl.ds(p * CX + CX - 8, 8), :]

    @pl.when(passes_on)
    def _():
        half_copies[1].start()

    def state_copy(n):
        return pltpu.make_async_remote_copy(
            chain.at[n], coarse.at[chip], chain_ss.at[n], chain_rs.at[chip],
            device_id=(n, space), device_id_type=MESH,
        )

    def state_arrival(p):
        return pltpu.make_async_remote_copy(
            chain.at[0], coarse.at[p], chain_ss.at[0], chain_rs.at[p],
            device_id=(tm, space), device_id_type=MESH,
        )

    @pl.when(is_owner)
    def _():
        jumps_mid[tm] = jump_mid[chip]
        jumps_edge[tm] = jump_edge[chip]

        def link(n, values):
            @pl.when(n != tm)
            def _():
                for i in range(2):
                    jump_arrival(n, i).wait_recv()

            own = jnp.concatenate(
                [jumps_edge[n, 0:8], jumps_mid[n], jumps_edge[n, 8:16]], axis=0
            )
            values = own + jnp.where(n > 0, 1.0, 0.0) * apply_coarse(chip, values)
            chain[n + 1] = values

            @pl.when(n + 1 != tm)
            def _():
                state_copy(n + 1).start()

            @pl.when(n + 1 == tm)
            def _():
                coarse[chip] = values

            return values

        lax.fori_loop(0, SLICES - 1, link, jnp.zeros((CX, TILE), F32))

    @pl.when(tm == 0)
    def _():
        coarse[...] = coarse_starts[...]

    stores = [
        pltpu.make_async_copy(half.at[pl.ds(p * CX, CX), :], half_out.at[p], store_sem.at[0, p])
        for p in range(PLACES)
    ]
    for store in stores:
        store.start()

    for p in range(PLACES):
        @pl.when(jnp.logical_and(tm > 0, tm != 2 * p))
        def _(p=p):
            state_arrival(p).wait_recv()

        stores.append(pltpu.make_async_copy(coarse.at[p], coarse_out.at[p], store_sem.at[1, p]))
        stores[-1].start()
        sums[p] = apply_coarse(p, coarse[p]) + mean[pl.ds(p * CX, CX), :]
        stores.append(pltpu.make_async_copy(sums.at[p], sum_out.at[p], store_sem.at[2, p]))
        stores[-1].start()

    @pl.when(tm > 0)
    def _():
        for copy in half_copies:
            copy.wait_recv()
        prev_stores = [
            pltpu.make_async_copy(src, prev_out.at[:, rows, :], store_sem.at[3, i])
            for i, (src, rows) in enumerate(
                [(prev_mid, pl.ds(8, MID)), (prev_edge.at[:, 0:8], pl.ds(0, 8)),
                 (prev_edge.at[:, 8:16], pl.ds(CX - 8, 8))]
            )
        ]
        for store in prev_stores:
            store.start()
        for store in prev_stores:
            store.wait()

    for store in stores:
        store.wait()

    for p in range(PLACES):
        @pl.when(sends_to(p))
        def _(p=p):
            for i in range(2):
                jump_copy(p, i).wait_send()

    @pl.when(passes_on)
    def _():
        for copy in half_copies:
            copy.wait_send()

    @pl.when(is_owner)
    def _():
        def sent(n, carry):
            @pl.when(n != tm)
            def _():
                state_copy(n).wait_send()

            return carry

        lax.fori_loop(1, SLICES, sent, 0)


def finish_kernel(
    neighbors_hbm, starts_hbm, sums_hbm, coarse_hbm, half_hbm, prev_hbm, ends_hbm, step_hbm,
    neighbors, starts, sums, coarse, half, prev, ends, step, load_sem, store_sem,
):
    loads = [
        pltpu.make_async_copy(src, dst, load_sem.at[i])
        for i, (src, dst) in enumerate(
            [(neighbors_hbm, neighbors), (sums_hbm, sums), (half_hbm, half),
             (coarse_hbm, coarse), (prev_hbm, prev), (starts_hbm, starts)]
        )
    ]
    for load in loads:
        load.start()
    later = lax.axis_index("tm") > 0
    even, odd = pl.ds(0, CX, stride=2), pl.ds(1, CX, stride=2)
    for load in loads[:3]:
        load.wait()
    order = place_order(neighbors, lax.axis_index("space"))
    stores = []
    for p in range(PLACES):
        t = order[p]
        total, difference = sums[p], half[p]
        ends[p, even, :] = total + difference
        ends[p, odd, :] = total - difference
        stores.append(pltpu.make_async_copy(ends.at[p], ends_hbm.at[t], store_sem.at[0, p]))
        stores[-1].start()
    for load in loads[3:]:
        load.wait()
    for p in range(PLACES):
        t = order[p]
        total, difference = coarse[p], prev[p]
        step[p, even, :] = jnp.where(later, total + difference - starts[t, even, :], 0.0)
        step[p, odd, :] = jnp.where(later, total - difference - starts[t, odd, :], 0.0)
        stores.append(pltpu.make_async_copy(step.at[p], step_hbm.at[t], store_sem.at[1, p]))
        stores[-1].start()
    for store in stores:
        store.wait()


def on_device(
    starts, diffusivity, velocity, obstacle, substep_scale, neighbors, coarse_x, coarse_y
):
    anywhere = pl.BlockSpec(memory_space=pl.ANY)
    tiles = (PLACES, TILE, TILE)
    places = jax.ShapeDtypeStruct((PLACES, CX, TILE), F32)
    dma = pltpu.SemaphoreType.DMA
    starts = starts[0]
    neighbors = neighbors.T
    sums, coarse, half, prev = pl.pallas_call(
        fine_kernel,
        out_shape=(places,) * 4,
        in_specs=[anywhere] * 8,
        out_specs=(anywhere,) * 4,
        scratch_shapes=[
            pltpu.SMEM((SUB,), F32),
            pltpu.SMEM((4, PLACES), jnp.int32),
            pltpu.VMEM((PLACES, 32, TILE), F32),
            pltpu.VMEM((PLACES, 32, TILE), F32),
            pltpu.VMEM((2, PLACES, 32, TILE), F32),
            pltpu.VMEM((PLACES, 32, TILE), jnp.int32),
            pltpu.VMEM((PLACES, TILE - 32, TILE), F32),
            pltpu.VMEM((PLACES, TILE - 32, TILE), F32),
            pltpu.VMEM((2, PLACES, TILE - 32, TILE), F32),
            pltpu.VMEM((PLACES, TILE - 32, TILE), jnp.int32),
            pltpu.VMEM((PLACES, CX, CX), F32),
            pltpu.VMEM(tiles, F32),
            dma((16,)),
            dma((4, PLACES)),
            pltpu.VMEM((TILE * 8 + 8, TILE), F32),
            pltpu.VMEM((TILE * 8, TILE), F32),
            pltpu.VMEM((TILE * 8, TILE), F32),
            pltpu.VMEM((TILE * 8, TILE), F32),
            pltpu.VMEM((4, 2 * SUB, 8, TILE), F32),
            pltpu.VMEM((4, 2 * SUB, 8, TILE), F32),
            pltpu.VMEM((SUB, 2, 8, TILE), F32),
            pltpu.VMEM((SUB, 2, 8, TILE), F32),
            pltpu.VMEM((PLACES, CX, CX), BF16),
            pltpu.VMEM((PLACES, CX, CX), BF16),
            pltpu.VMEM(tiles, BF16),
            pltpu.VMEM(tiles, BF16),
            pltpu.VMEM((PLACES, CX, TILE), F32),
            pltpu.VMEM((PLACES * CX, TILE), F32),
            pltpu.VMEM((PLACES * CX, TILE), F32),
            pltpu.VMEM((PLACES * CX, TILE), F32),
            pltpu.VMEM((PLACES, MID, TILE), F32),
            pltpu.VMEM((PLACES, 16, TILE), F32),
            pltpu.VMEM((PLACES, MID, TILE), F32),
            pltpu.VMEM((PLACES, 16, TILE), F32),
            pltpu.VMEM((PLACES, MID, TILE), F32),
            pltpu.VMEM((PLACES, 16, TILE), F32),
            pltpu.VMEM((SLICES, MID, TILE), F32),
            pltpu.VMEM((SLICES, 16, TILE), F32),
            pltpu.VMEM((SLICES, CX, TILE), F32),
            pltpu.VMEM((PLACES, CX, TILE), F32),
            pltpu.VMEM((PLACES, CX, TILE), F32),
            dma((2,)),
            dma((2,)),
            dma((2, PLACES)),
            dma((2, SLICES)),
            dma((2,)),
            dma((2,)),
            dma((SLICES,)),
            dma((PLACES,)),
        ],
        compiler_params=pltpu.CompilerParams(
            collective_id=0, has_side_effects=True, vmem_limit_bytes=60 << 20
        ),
    )(substep_scale, neighbors, starts, diffusivity, velocity, obstacle, coarse_x, coarse_y)
    ends, step = pl.pallas_call(
        finish_kernel,
        out_shape=(jax.ShapeDtypeStruct(tiles, F32),) * 2,
        in_specs=[anywhere] * 6,
        out_specs=(anywhere, anywhere),
        scratch_shapes=[pltpu.SMEM((4, PLACES), jnp.int32), pltpu.VMEM(tiles, F32)]
        + [pltpu.VMEM((PLACES, CX, TILE), F32)] * 4
        + [pltpu.VMEM(tiles, F32)] * 2
        + [dma((6,)), dma((2, PLACES))],
        compiler_params=pltpu.CompilerParams(vmem_limit_bytes=60 << 20),
    )(neighbors, starts, sums, coarse, half, prev)
    return ends[None], step[None]


def solution(mesh):
    placed = (
        P("tm", "space", None, None),
        P("space", None, None),
        P(None, "space", None, None),
        P("space", None, None),
        P(),
        P("space", None),
        P("space", None, None),
        P("space", None, None),
    )
    return jax.shard_map(
        on_device,
        mesh=mesh,
        in_specs=placed,
        out_specs=(P("tm", "space", None, None), P("tm", "space", None, None)),
        check_vma=False,
    )
```

```python
import jax
import jax.numpy as jnp
from jax import lax
from jax.experimental import pallas as pl
from jax.experimental.pallas import tpu as pltpu
from jax.sharding import PartitionSpec as P

MESH = pl.DeviceIdType.MESH
SUB = 12
PLACES = 8
TILE = 128
CX = 64
MID = 48
SLICES = 16
F32 = jnp.float32
BF16 = jnp.bfloat16


def halves(value):
    high = value.astype(BF16)
    return high, (value - high.astype(F32)).astype(BF16)


def product(left, right):
    left_high, left_low = left
    right_high, right_low = right
    total = jnp.dot(left_high, right_low, preferred_element_type=F32)
    total = total + jnp.dot(left_low, right_high, preferred_element_type=F32)
    return total + jnp.dot(left_high, right_high, preferred_element_type=F32)


def place_order(neighbors, space):
    first = jnp.int32(0)
    for t in range(PLACES):
        first = first + jnp.where(neighbors[2, t] == PLACES * 8, t, 0)
    first = jnp.clip(first, 0, PLACES - 1)
    order = [first]
    for _ in range(PLACES - 1):
        order.append(jnp.clip(neighbors[3, order[-1]] - space * PLACES, 0, PLACES - 1))
    return order


def fine_kernel(
    scale_hbm, neighbors_hbm, starts_hbm, diff_hbm, vel_hbm, obst_hbm, cx_hbm, cy_hbm,
    sum_out, coarse_out, half_out, prev_out,
    scale, neighbors, starts_edge, diff_edge, vel_edge, obst_edge, starts, diff, vel, obst,
    cx, cy, load_sem,
    state, coef_d, coef_a, coef_b, west, east, west_past, east_past,
    xh, xl, yh, yl, coarse_starts, coarse_ends, mean, half,
    jump_mid, jump_edge, half_mid, half_edge, prev_mid, prev_edge, jumps_mid, jumps_edge,
    chain, coarse,
    halo_ss, halo_rs, jump_ss, jump_rs, half_ss, half_rs, chain_ss, chain_rs,
):
    tm = lax.axis_index("tm")
    space = lax.axis_index("space")
    core = lax.rem(tm, 2)
    chip = tm // 2
    is_owner = core == 0

    fields = (starts_hbm, diff_hbm, obst_hbm, vel_hbm)
    edges = (starts_edge, diff_edge, obst_edge, vel_edge)
    inner = (starts, diff, obst, vel)
    pairs = [(neighbors_hbm, neighbors), (scale_hbm, scale)]
    for first, at in ((0, 0), (TILE - 16, 16)):
        pairs += [
            (src.at[..., pl.ds(first, 16), :], dst.at[..., pl.ds(at, 16), :])
            for src, dst in zip(fields, edges)
        ]
    pairs += [
        (src.at[..., pl.ds(16, TILE - 32), :], dst) for src, dst in zip(fields, inner)
    ]
    pairs += [(cx_hbm, cx), (cy_hbm, cy)]
    loads = [
        pltpu.make_async_copy(src, dst, load_sem.at[i]) for i, (src, dst) in enumerate(pairs)
    ]
    for load in loads:
        load.start()

    barrier = pltpu.get_barrier_semaphore()

    def greet(target_tm, target_space):
        pl.semaphore_signal(
            barrier, inc=1, device_id=(target_tm, target_space), device_id_type=MESH
        )

    @pl.when(space > 0)
    def _():
        greet(tm, space - 1)

    @pl.when(space < 7)
    def _():
        greet(tm, space + 1)

    def greet_slice(i, carry):
        greet(lax.rem(tm + i, SLICES), space)
        return carry

    lax.fori_loop(1, SLICES, greet_slice, 0)

    def convert(p, block, at, sources):
        first, diffusion, tubes, speed = sources
        rows = pl.ds(at if isinstance(at, int) else pl.multiple_of(at, 8), 8)
        spread = pl.ds(block * 64 + p, 8, stride=8)
        t = order[p]
        open_cells = 1.0 - tubes[t, rows, :].astype(F32)
        state[spread, :] = first[t, rows, :]
        coef_d[spread, :] = open_cells * diffusion[t, rows, :]
        coef_a[spread, :] = (0.5 * open_cells) * speed[0, t, rows, :]
        coef_b[spread, :] = (0.5 * open_cells) * speed[1, t, rows, :]

    for load in loads[:10]:
        load.wait()
    order = place_order(neighbors, space)
    for p in range(PLACES):
        for i, block in enumerate((0, 1, TILE // 8 - 2, TILE // 8 - 1)):
            convert(p, block, 8 * i, edges)

    def row(ref, r):
        at = r * 8 if isinstance(r, int) else pl.multiple_of(r * 8, 8)
        return ref[pl.ds(at, 8), :]

    for q, ref in enumerate((state, coef_d, coef_a, coef_b)):
        for i in range(SUB):
            west[q, SUB + i] = row(ref, i)
            east[q, i] = row(ref, TILE - SUB + i)

    @pl.when(space == 0)
    def _():
        west[:, 0:SUB] = jnp.zeros((4, SUB, 8, TILE), F32)

    @pl.when(space == 7)
    def _():
        east[:, SUB : 2 * SUB] = jnp.zeros((4, SUB, 8, TILE), F32)

    greeted = SLICES - 1 + jnp.where(space > 0, 1, 0) + jnp.where(space < 7, 1, 0)

    to_west = pltpu.make_async_remote_copy(
        west.at[:, SUB : 2 * SUB], east.at[:, SUB : 2 * SUB], halo_ss.at[0], halo_rs.at[1],
        device_id=(tm, jnp.maximum(space - 1, 0)), device_id_type=MESH,
    )
    to_east = pltpu.make_async_remote_copy(
        east.at[:, 0:SUB], west.at[:, 0:SUB], halo_ss.at[1], halo_rs.at[0],
        device_id=(tm, jnp.minimum(space + 1, 7)), device_id_type=MESH,
    )

    lane = lax.broadcasted_iota(jnp.int32, (8, TILE), 1)
    sub = lax.broadcasted_iota(jnp.int32, (8, TILE), 0)
    south_face = lane == 0
    north_face = lane == TILE - 1
    north_wrap = jnp.logical_and(north_face, sub == 0)
    south_wrap = jnp.logical_and(south_face, sub == 7)

    def update(before, now, after, d, a, b, strength):
        south = jnp.where(north_face, pltpu.roll(now, 1, 0), now)
        south = pltpu.roll(jnp.where(north_wrap, 0.0, south), 1, 1)
        north = jnp.where(south_face, pltpu.roll(now, 7, 0), now)
        north = pltpu.roll(jnp.where(south_wrap, 0.0, north), TILE - 1, 1)
        laplace = (before + after) + (south + north) - 4.0 * now
        return now + (strength * d) * laplace - a * (after - before) - b * (north - south)

    pl.semaphore_wait(barrier, greeted)

    @pl.when(space > 0)
    def _():
        to_west.start()

    @pl.when(space < 7)
    def _():
        to_east.start()

    for load in loads[10:]:
        load.wait()
    state[pl.ds(TILE * 8, 8), :] = jnp.zeros((8, TILE), F32)
    for p in range(PLACES):

        def convert_inner(i, carry, p=p):
            convert(p, i + 2, i * 8, inner)
            return carry

        lax.fori_loop(0, TILE // 8 - 4, convert_inner, 0, unroll=4)

    for p in range(PLACES):
        t = order[p]
        x_high, x_low = halves(cx[t])
        xh[p] = x_high
        xl[p] = x_low
        y_high, y_low = halves(cy[t].T)
        yh[p] = y_high
        yl[p] = y_low
        for ref, at, target in (
            (starts_edge, 0, slice(0, 8)),
            (starts_edge, 16, slice(CX - 8, CX)),
            (starts, 0, slice(8, CX - 8)),
        ):
            count = target.stop - target.start
            coarse_starts[p, target] = 0.5 * (
                ref[t, pl.ds(at, count, stride=2), :] + ref[t, pl.ds(at + 1, count, stride=2), :]
            )

    def apply_coarse(p, values):
        mixed = product((xh[p], xl[p]), halves(values))
        return product(halves(mixed), (yh[p], yl[p]))

    for p in range(PLACES):
        coarse_ends[pl.ds(p * CX, CX), :] = apply_coarse(p, coarse_starts[p])

    def substep(s, carry):
        strength = scale[s]
        west_past[s, 0] = row(state, s)
        west_past[s, 1] = row(state, s + 1)
        east_past[s, 0] = row(state, TILE - 1 - s)
        east_past[s, 1] = row(state, TILE - 2 - s)
        before = jnp.zeros((8, TILE), F32)
        now = row(state, 0)
        for r in range(TILE):
            after = row(state, r + 1)
            state[r * 8 : r * 8 + 8, :] = update(
                before, now, after, row(coef_d, r), row(coef_a, r), row(coef_b, r), strength
            )
            before, now = now, after

        @pl.when(s == 0)
        def _():
            for r in range(TILE):
                here = slice(r * 8, r * 8 + 8)
                state[here, :] = jnp.where(coef_d[here, :] > 0.0, state[here, :], 0.0)

        return carry

    lax.fori_loop(0, SUB, substep, 0)

    first_slice = jnp.where(tm == 0, 1.0, 0.0)

    def settle(i, even, odd):
        spread = pl.ds(i, 8, stride=CX)
        middle = 0.5 * (even + odd)
        coarse_end = coarse_ends[spread, :]
        mean[spread, :] = middle - coarse_end
        half[spread, :] = 0.5 * (even - odd)

    def settle_inner(i, carry):
        settle(i, row(state, 2 * i), row(state, 2 * i + 1))
        return carry

    lax.fori_loop(SUB // 2, CX - SUB // 2, settle_inner, 0, unroll=4)

    jump_parts = ((jump_mid, jumps_mid), (jump_edge, jumps_edge))

    def jump_copy(p, i):
        source, target = jump_parts[i]
        return pltpu.make_async_remote_copy(
            source.at[p], target.at[tm], jump_ss.at[i, p], jump_rs.at[i, tm],
            device_id=(2 * p, space), device_id_type=MESH,
        )

    def jump_arrival(n, i):
        source, target = jump_parts[i]
        return pltpu.make_async_remote_copy(
            source.at[0], target.at[n], jump_ss.at[i, 0], jump_rs.at[i, n],
            device_id=(tm, space), device_id_type=MESH,
        )

    half_copies = [
        pltpu.make_async_remote_copy(
            source, target, half_ss.at[i], half_rs.at[i],
            device_id=(jnp.minimum(tm + 1, SLICES - 1), space), device_id_type=MESH,
        )
        for i, (source, target) in enumerate(((half_mid, prev_mid), (half_edge, prev_edge)))
    ]
    passes_on = tm < SLICES - 1

    def sends_to(p):
        return jnp.logical_and(tm != 2 * p, passes_on)

    for p in range(PLACES):
        rows = pl.ds(p * CX + 8, MID)
        jump_mid[p] = mean[rows, :] + first_slice * coarse_ends[rows, :]

        @pl.when(sends_to(p))
        def _(p=p):
            jump_copy(p, 0).start()

    for p in range(PLACES):
        half_mid[p] = half[pl.ds(p * CX + 8, MID), :]

    @pl.when(passes_on)
    def _():
        half_copies[0].start()

    @pl.when(space > 0)
    def _():
        to_west.wait_send()
        to_east.wait_recv()

    @pl.when(space < 7)
    def _():
        to_east.wait_send()
        to_west.wait_recv()

    def border(s, carry):
        strength = scale[s]
        low, high = carry[:SUB], carry[SUB:]
        low = low + (west_past[s, 0], west_past[s, 1])
        high = high + (east_past[s, 0], east_past[s, 1])
        fresh_low, fresh_high = [], []
        for w in range(SUB):
            at = s + 1 + w
            fresh = update(
                low[w], low[w + 1], low[w + 2], west[1, at], west[2, at], west[3, at], strength
            )
            fresh_low.append(jnp.where(west[1, at] > 0.0, fresh, 0.0))
            at = 2 * SUB - 2 - s - w
            fresh = update(
                high[w + 2], high[w + 1], high[w], east[1, at], east[2, at], east[3, at], strength
            )
            fresh_high.append(jnp.where(east[1, at] > 0.0, fresh, 0.0))
        return tuple(fresh_low) + tuple(fresh_high)

    edge_rows = lax.fori_loop(
        0, SUB, border,
        tuple(west[0, w] for w in range(SUB))
        + tuple(east[0, 2 * SUB - 1 - w] for w in range(SUB)),
    )
    low, high = edge_rows[:SUB], edge_rows[SUB:][::-1]
    for i in range(SUB // 2):
        settle(i, low[2 * i], low[2 * i + 1])
        settle(CX - SUB // 2 + i, high[2 * i], high[2 * i + 1])

    for p in range(PLACES):
        for at, first in ((0, 0), (8, CX - 8)):
            rows = pl.ds(p * CX + first, 8)
            jump_edge[p, at : at + 8] = mean[rows, :] + first_slice * coarse_ends[rows, :]

        @pl.when(sends_to(p))
        def _(p=p):
            jump_copy(p, 1).start()

    for p in range(PLACES):
        half_edge[p, 0:8] = half[pl.ds(p * CX, 8), :]
        half_edge[p, 8:16] = half[pl.ds(p * CX + CX - 8, 8), :]

    @pl.when(passes_on)
    def _():
        half_copies[1].start()

    def state_copy(n):
        return pltpu.make_async_remote_copy(
            chain.at[n], coarse.at[chip], chain_ss.at[n], chain_rs.at[chip],
            device_id=(n, space), device_id_type=MESH,
        )

    def state_arrival(p):
        return pltpu.make_async_remote_copy(
            chain.at[0], coarse.at[p], chain_ss.at[0], chain_rs.at[p],
            device_id=(tm, space), device_id_type=MESH,
        )

    @pl.when(is_owner)
    def _():
        jumps_mid[tm] = jump_mid[chip]
        jumps_edge[tm] = jump_edge[chip]

        def link(n, values):
            @pl.when(n != tm)
            def _():
                for i in range(2):
                    jump_arrival(n, i).wait_recv()

            own = jnp.concatenate(
                [jumps_edge[n, 0:8], jumps_mid[n], jumps_edge[n, 8:16]], axis=0
            )
            values = own + jnp.where(n > 0, 1.0, 0.0) * apply_coarse(chip, values)
            chain[n + 1] = values

            @pl.when(n + 1 != tm)
            def _():
                state_copy(n + 1).start()

            @pl.when(n + 1 == tm)
            def _():
                coarse[chip] = values

            return values

        lax.fori_loop(0, SLICES - 1, link, jnp.zeros((CX, TILE), F32))

    @pl.when(tm == 0)
    def _():
        coarse[...] = coarse_starts[...]

    for p in range(PLACES):
        half_out[p] = half[pl.ds(p * CX, CX), :]

    for p in range(PLACES):
        @pl.when(jnp.logical_and(tm > 0, tm != 2 * p))
        def _(p=p):
            state_arrival(p).wait_recv()

        values = coarse[p]
        coarse_out[p] = values
        sum_out[p] = apply_coarse(p, values) + mean[pl.ds(p * CX, CX), :]

    @pl.when(tm > 0)
    def _():
        for copy in half_copies:
            copy.wait_recv()
        for p in range(PLACES):
            prev_out[p, 0:8] = prev_edge[p, 0:8]
            prev_out[p, 8 : CX - 8] = prev_mid[p]
            prev_out[p, CX - 8 : CX] = prev_edge[p, 8:16]

    for p in range(PLACES):
        @pl.when(sends_to(p))
        def _(p=p):
            for i in range(2):
                jump_copy(p, i).wait_send()

    @pl.when(passes_on)
    def _():
        for copy in half_copies:
            copy.wait_send()

    @pl.when(is_owner)
    def _():
        def sent(n, carry):
            @pl.when(n != tm)
            def _():
                state_copy(n).wait_send()

            return carry

        lax.fori_loop(1, SLICES, sent, 0)


def finish_kernel(
    neighbors_hbm, starts_hbm, sums, coarse, half, prev, ends_hbm, step_hbm,
    neighbors, starts, ends, step, load_sem, store_sem,
):
    loads = [
        pltpu.make_async_copy(src, dst, load_sem.at[i])
        for i, (src, dst) in enumerate(
            [(neighbors_hbm, neighbors), (starts_hbm, starts)]
        )
    ]
    for load in loads:
        load.start()
    later = lax.axis_index("tm") > 0
    even, odd = pl.ds(0, CX, stride=2), pl.ds(1, CX, stride=2)
    loads[0].wait()
    order = place_order(neighbors, lax.axis_index("space"))
    stores = []
    for p in range(PLACES):
        t = order[p]
        total, difference = sums[p], half[p]
        ends[p, even, :] = total + difference
        ends[p, odd, :] = total - difference
        stores.append(pltpu.make_async_copy(ends.at[p], ends_hbm.at[t], store_sem.at[0, p]))
        stores[-1].start()
    loads[1].wait()
    for p in range(PLACES):
        t = order[p]
        total, difference = coarse[p], prev[p]
        step[p, even, :] = jnp.where(later, total + difference - starts[t, even, :], 0.0)
        step[p, odd, :] = jnp.where(later, total - difference - starts[t, odd, :], 0.0)
        stores.append(pltpu.make_async_copy(step.at[p], step_hbm.at[t], store_sem.at[1, p]))
        stores[-1].start()
    for store in stores:
        store.wait()


def on_device(
    starts, diffusivity, velocity, obstacle, substep_scale, neighbors, coarse_x, coarse_y
):
    anywhere = pl.BlockSpec(memory_space=pltpu.HBM)
    vmem = pl.BlockSpec(memory_space=pltpu.VMEM)
    tiles = (PLACES, TILE, TILE)
    places = pltpu.VMEM((PLACES, CX, TILE), F32)
    dma = pltpu.SemaphoreType.DMA
    starts = starts[0]
    in_hbm = lambda x: pltpu.with_memory_space_constraint(x, pltpu.HBM)
    neighbors = neighbors.T
    sums, coarse, half, prev = pl.pallas_call(
        fine_kernel,
        out_shape=(places,) * 4,
        in_specs=[anywhere] * 8,
        out_specs=(vmem,) * 4,
        scratch_shapes=[
            pltpu.SMEM((SUB,), F32),
            pltpu.SMEM((4, PLACES), jnp.int32),
            pltpu.VMEM((PLACES, 32, TILE), F32),
            pltpu.VMEM((PLACES, 32, TILE), F32),
            pltpu.VMEM((2, PLACES, 32, TILE), F32),
            pltpu.VMEM((PLACES, 32, TILE), jnp.int32),
            pltpu.VMEM((PLACES, TILE - 32, TILE), F32),
            pltpu.VMEM((PLACES, TILE - 32, TILE), F32),
            pltpu.VMEM((2, PLACES, TILE - 32, TILE), F32),
            pltpu.VMEM((PLACES, TILE - 32, TILE), jnp.int32),
            pltpu.VMEM((PLACES, CX, CX), F32),
            pltpu.VMEM(tiles, F32),
            dma((16,)),
            pltpu.VMEM((TILE * 8 + 8, TILE), F32),
            pltpu.VMEM((TILE * 8, TILE), F32),
            pltpu.VMEM((TILE * 8, TILE), F32),
            pltpu.VMEM((TILE * 8, TILE), F32),
            pltpu.VMEM((4, 2 * SUB, 8, TILE), F32),
            pltpu.VMEM((4, 2 * SUB, 8, TILE), F32),
            pltpu.VMEM((SUB, 2, 8, TILE), F32),
            pltpu.VMEM((SUB, 2, 8, TILE), F32),
            pltpu.VMEM((PLACES, CX, CX), BF16),
            pltpu.VMEM((PLACES, CX, CX), BF16),
            pltpu.VMEM(tiles, BF16),
            pltpu.VMEM(tiles, BF16),
            pltpu.VMEM((PLACES, CX, TILE), F32),
            pltpu.VMEM((PLACES * CX, TILE), F32),
            pltpu.VMEM((PLACES * CX, TILE), F32),
            pltpu.VMEM((PLACES * CX, TILE), F32),
            pltpu.VMEM((PLACES, MID, TILE), F32),
            pltpu.VMEM((PLACES, 16, TILE), F32),
            pltpu.VMEM((PLACES, MID, TILE), F32),
            pltpu.VMEM((PLACES, 16, TILE), F32),
            pltpu.VMEM((PLACES, MID, TILE), F32),
            pltpu.VMEM((PLACES, 16, TILE), F32),
            pltpu.VMEM((SLICES, MID, TILE), F32),
            pltpu.VMEM((SLICES, 16, TILE), F32),
            pltpu.VMEM((SLICES, CX, TILE), F32),
            pltpu.VMEM((PLACES, CX, TILE), F32),
            dma((2,)),
            dma((2,)),
            dma((2, PLACES)),
            dma((2, SLICES)),
            dma((2,)),
            dma((2,)),
            dma((SLICES,)),
            dma((PLACES,)),
        ],
        compiler_params=pltpu.CompilerParams(
            collective_id=0, has_side_effects=True, vmem_limit_bytes=32 << 20
        ),
    )(*map(in_hbm, (substep_scale, neighbors, starts, diffusivity, velocity, obstacle, coarse_x, coarse_y)))
    ends, step = pl.pallas_call(
        finish_kernel,
        out_shape=(jax.ShapeDtypeStruct(tiles, F32),) * 2,
        in_specs=[anywhere] * 2 + [vmem] * 4,
        out_specs=(anywhere, anywhere),
        scratch_shapes=[pltpu.SMEM((4, PLACES), jnp.int32), pltpu.VMEM(tiles, F32)]
        + [pltpu.VMEM(tiles, F32)] * 2
        + [dma((2,)), dma((2, PLACES))],
        compiler_params=pltpu.CompilerParams(vmem_limit_bytes=32 << 20),
    )(in_hbm(neighbors), in_hbm(starts), sums, coarse, half, prev)
    return ends[None], step[None]


def solution(mesh):
    placed = (
        P("tm", "space", None, None),
        P("space", None, None),
        P(None, "space", None, None),
        P("space", None, None),
        P(),
        P("space", None),
        P("space", None, None),
        P("space", None, None),
    )
    return jax.shard_map(
        on_device,
        mesh=mesh,
        in_specs=placed,
        out_specs=(P("tm", "space", None, None), P("tm", "space", None, None)),
        check_vma=False,
    )
```

```python
import jax
import jax.numpy as jnp
from jax import lax
from jax.experimental import pallas as pl
from jax.experimental.pallas import tpu as pltpu
from jax.sharding import PartitionSpec as P

MESH = pl.DeviceIdType.MESH
SUB = 12
PLACES = 8
TILE = 128
CX = 64
MID = 48
SLICES = 16
F32 = jnp.float32
BF16 = jnp.bfloat16


def halves(value):
    high = value.astype(BF16)
    return high, (value - high.astype(F32)).astype(BF16)


def product(left, right):
    left_high, left_low = left
    right_high, right_low = right
    total = jnp.dot(left_high, right_low, preferred_element_type=F32)
    total = total + jnp.dot(left_low, right_high, preferred_element_type=F32)
    return total + jnp.dot(left_high, right_high, preferred_element_type=F32)


def place_order(neighbors, space):
    first = jnp.int32(0)
    for t in range(PLACES):
        first = first + jnp.where(neighbors[2, t] == PLACES * 8, t, 0)
    first = jnp.clip(first, 0, PLACES - 1)
    order = [first]
    for _ in range(PLACES - 1):
        order.append(jnp.clip(neighbors[3, order[-1]] - space * PLACES, 0, PLACES - 1))
    return order


def fine_kernel(
    scale_hbm, neighbors_hbm, starts_hbm, diff_hbm, vel_hbm, obst_hbm, cx_hbm, cy_hbm,
    sum_out, coarse_out, half_out, even_out, odd_out,
    scale, neighbors, starts_edge, diff_edge, vel_edge, obst_edge, starts, diff, vel, obst,
    cx, cy, load_sem,
    state, coef_d, coef_a, coef_b, west, east, west_past, east_past,
    xh, xl, yh, yl, coarse_starts, coarse_ends, mean, half,
    jump_mid, jump_edge, half_mid, half_edge, prev_mid, prev_edge, jumps_mid, jumps_edge,
    chain, coarse, mean_place,
    halo_ss, halo_rs, jump_ss, jump_rs, half_ss, half_rs, chain_ss, chain_rs,
):
    tm = lax.axis_index("tm")
    space = lax.axis_index("space")
    core = lax.rem(tm, 2)
    chip = tm // 2
    is_owner = core == 0

    fields = (starts_hbm, diff_hbm, obst_hbm, vel_hbm)
    edges = (starts_edge, diff_edge, obst_edge, vel_edge)
    inner = (starts, diff, obst, vel)
    pairs = [(neighbors_hbm, neighbors), (scale_hbm, scale)]
    for first, at in ((0, 0), (TILE - 16, 16)):
        pairs += [
            (src.at[..., pl.ds(first, 16), :], dst.at[..., pl.ds(at, 16), :])
            for src, dst in zip(fields, edges)
        ]
    pairs += [
        (src.at[..., pl.ds(16, TILE - 32), :], dst) for src, dst in zip(fields, inner)
    ]
    pairs += [(cx_hbm, cx), (cy_hbm, cy)]
    loads = [
        pltpu.make_async_copy(src, dst, load_sem.at[i]) for i, (src, dst) in enumerate(pairs)
    ]
    for load in loads:
        load.start()

    barrier = pltpu.get_barrier_semaphore()

    def greet(target_tm, target_space):
        pl.semaphore_signal(
            barrier, inc=1, device_id=(target_tm, target_space), device_id_type=MESH
        )

    @pl.when(space > 0)
    def _():
        greet(tm, space - 1)

    @pl.when(space < 7)
    def _():
        greet(tm, space + 1)

    def greet_slice(i, carry):
        greet(lax.rem(tm + i, SLICES), space)
        return carry

    lax.fori_loop(1, SLICES, greet_slice, 0)

    def convert(p, block, at, sources):
        first, diffusion, tubes, speed = sources
        rows = pl.ds(at if isinstance(at, int) else pl.multiple_of(at, 8), 8)
        spread = pl.ds(block * 64 + p, 8, stride=8)
        t = order[p]
        open_cells = 1.0 - tubes[t, rows, :].astype(F32)
        state[spread, :] = first[t, rows, :]
        coef_d[spread, :] = open_cells * diffusion[t, rows, :]
        coef_a[spread, :] = (0.5 * open_cells) * speed[0, t, rows, :]
        coef_b[spread, :] = (0.5 * open_cells) * speed[1, t, rows, :]

    for load in loads[:10]:
        load.wait()
    order = place_order(neighbors, space)
    for p in range(PLACES):
        for i, block in enumerate((0, 1, TILE // 8 - 2, TILE // 8 - 1)):
            convert(p, block, 8 * i, edges)

    def row(ref, r):
        at = r * 8 if isinstance(r, int) else pl.multiple_of(r * 8, 8)
        return ref[pl.ds(at, 8), :]

    for q, ref in enumerate((state, coef_d, coef_a, coef_b)):
        for i in range(SUB):
            west[q, SUB + i] = row(ref, i)
            east[q, i] = row(ref, TILE - SUB + i)

    @pl.when(space == 0)
    def _():
        west[:, 0:SUB] = jnp.zeros((4, SUB, 8, TILE), F32)

    @pl.when(space == 7)
    def _():
        east[:, SUB : 2 * SUB] = jnp.zeros((4, SUB, 8, TILE), F32)

    greeted = SLICES - 1 + jnp.where(space > 0, 1, 0) + jnp.where(space < 7, 1, 0)

    to_west = pltpu.make_async_remote_copy(
        west.at[:, SUB : 2 * SUB], east.at[:, SUB : 2 * SUB], halo_ss.at[0], halo_rs.at[1],
        device_id=(tm, jnp.maximum(space - 1, 0)), device_id_type=MESH,
    )
    to_east = pltpu.make_async_remote_copy(
        east.at[:, 0:SUB], west.at[:, 0:SUB], halo_ss.at[1], halo_rs.at[0],
        device_id=(tm, jnp.minimum(space + 1, 7)), device_id_type=MESH,
    )

    lane = lax.broadcasted_iota(jnp.int32, (8, TILE), 1)
    sub = lax.broadcasted_iota(jnp.int32, (8, TILE), 0)
    south_face = lane == 0
    north_face = lane == TILE - 1
    north_wrap = jnp.logical_and(north_face, sub == 0)
    south_wrap = jnp.logical_and(south_face, sub == 7)

    def update(before, now, after, d, a, b, strength):
        south = jnp.where(north_face, pltpu.roll(now, 1, 0), now)
        south = pltpu.roll(jnp.where(north_wrap, 0.0, south), 1, 1)
        north = jnp.where(south_face, pltpu.roll(now, 7, 0), now)
        north = pltpu.roll(jnp.where(south_wrap, 0.0, north), TILE - 1, 1)
        laplace = (before + after) + (south + north) - 4.0 * now
        return now + (strength * d) * laplace - a * (after - before) - b * (north - south)

    pl.semaphore_wait(barrier, greeted)

    @pl.when(space > 0)
    def _():
        to_west.start()

    @pl.when(space < 7)
    def _():
        to_east.start()

    for load in loads[10:]:
        load.wait()
    state[pl.ds(TILE * 8, 8), :] = jnp.zeros((8, TILE), F32)
    for p in range(PLACES):

        def convert_inner(i, carry, p=p):
            convert(p, i + 2, i * 8, inner)
            return carry

        lax.fori_loop(0, TILE // 8 - 4, convert_inner, 0, unroll=4)

    for p in range(PLACES):
        t = order[p]
        x_high, x_low = halves(cx[t])
        xh[p] = x_high
        xl[p] = x_low
        y_high, y_low = halves(cy[t].T)
        yh[p] = y_high
        yl[p] = y_low
        for ref, at, target in (
            (starts_edge, 0, slice(0, 8)),
            (starts_edge, 16, slice(CX - 8, CX)),
            (starts, 0, slice(8, CX - 8)),
        ):
            count = target.stop - target.start
            coarse_starts[p, target] = 0.5 * (
                ref[t, pl.ds(at, count, stride=2), :] + ref[t, pl.ds(at + 1, count, stride=2), :]
            )

    def apply_coarse(p, values):
        mixed = product((xh[p], xl[p]), halves(values))
        return product(halves(mixed), (yh[p], yl[p]))

    for p in range(PLACES):
        coarse_ends[pl.ds(p * CX, CX), :] = apply_coarse(p, coarse_starts[p])

    def substep(s, carry):
        strength = scale[s]
        west_past[s, 0] = row(state, s)
        west_past[s, 1] = row(state, s + 1)
        east_past[s, 0] = row(state, TILE - 1 - s)
        east_past[s, 1] = row(state, TILE - 2 - s)
        before = jnp.zeros((8, TILE), F32)
        now = row(state, 0)
        for r in range(TILE):
            after = row(state, r + 1)
            state[r * 8 : r * 8 + 8, :] = update(
                before, now, after, row(coef_d, r), row(coef_a, r), row(coef_b, r), strength
            )
            before, now = now, after

        @pl.when(s == 0)
        def _():
            for r in range(TILE):
                here = slice(r * 8, r * 8 + 8)
                state[here, :] = jnp.where(coef_d[here, :] > 0.0, state[here, :], 0.0)

        return carry

    lax.fori_loop(0, SUB, substep, 0)

    first_slice = jnp.where(tm == 0, 1.0, 0.0)

    def settle(i, even, odd):
        spread = pl.ds(i, 8, stride=CX)
        middle = 0.5 * (even + odd)
        coarse_end = coarse_ends[spread, :]
        mean[spread, :] = middle - coarse_end
        half[spread, :] = 0.5 * (even - odd)

    def settle_inner(i, carry):
        settle(i, row(state, 2 * i), row(state, 2 * i + 1))
        return carry

    lax.fori_loop(SUB // 2, CX - SUB // 2, settle_inner, 0, unroll=4)

    jump_parts = ((jump_mid, jumps_mid), (jump_edge, jumps_edge))

    def jump_copy(p, i):
        source, target = jump_parts[i]
        return pltpu.make_async_remote_copy(
            source.at[p], target.at[tm], jump_ss.at[i, p], jump_rs.at[i, tm],
            device_id=(2 * p, space), device_id_type=MESH,
        )

    def jump_arrival(n, i):
        source, target = jump_parts[i]
        return pltpu.make_async_remote_copy(
            source.at[0], target.at[n], jump_ss.at[i, 0], jump_rs.at[i, n],
            device_id=(tm, space), device_id_type=MESH,
        )

    half_copies = [
        pltpu.make_async_remote_copy(
            source, target, half_ss.at[i], half_rs.at[i],
            device_id=(jnp.minimum(tm + 1, SLICES - 1), space), device_id_type=MESH,
        )
        for i, (source, target) in enumerate(((half_mid, prev_mid), (half_edge, prev_edge)))
    ]
    passes_on = tm < SLICES - 1

    def sends_to(p):
        return jnp.logical_and(tm != 2 * p, passes_on)

    for p in range(PLACES):
        rows = pl.ds(p * CX + 8, MID)
        jump_mid[p] = mean[rows, :] + first_slice * coarse_ends[rows, :]

        @pl.when(sends_to(p))
        def _(p=p):
            jump_copy(p, 0).start()

    for p in range(PLACES):
        half_mid[p] = half[pl.ds(p * CX + 8, MID), :]

    @pl.when(passes_on)
    def _():
        half_copies[0].start()

    @pl.when(space > 0)
    def _():
        to_west.wait_send()
        to_east.wait_recv()

    @pl.when(space < 7)
    def _():
        to_east.wait_send()
        to_west.wait_recv()

    def border(s, carry):
        strength = scale[s]
        low, high = carry[:SUB], carry[SUB:]
        low = low + (west_past[s, 0], west_past[s, 1])
        high = high + (east_past[s, 0], east_past[s, 1])
        fresh_low, fresh_high = [], []
        for w in range(SUB):
            at = s + 1 + w
            fresh = update(
                low[w], low[w + 1], low[w + 2], west[1, at], west[2, at], west[3, at], strength
            )
            fresh_low.append(jnp.where(west[1, at] > 0.0, fresh, 0.0))
            at = 2 * SUB - 2 - s - w
            fresh = update(
                high[w + 2], high[w + 1], high[w], east[1, at], east[2, at], east[3, at], strength
            )
            fresh_high.append(jnp.where(east[1, at] > 0.0, fresh, 0.0))
        return tuple(fresh_low) + tuple(fresh_high)

    edge_rows = lax.fori_loop(
        0, SUB, border,
        tuple(west[0, w] for w in range(SUB))
        + tuple(east[0, 2 * SUB - 1 - w] for w in range(SUB)),
    )
    low, high = edge_rows[:SUB], edge_rows[SUB:][::-1]
    for i in range(SUB // 2):
        settle(i, low[2 * i], low[2 * i + 1])
        settle(CX - SUB // 2 + i, high[2 * i], high[2 * i + 1])

    for p in range(PLACES):
        for at, first in ((0, 0), (8, CX - 8)):
            rows = pl.ds(p * CX + first, 8)
            jump_edge[p, at : at + 8] = mean[rows, :] + first_slice * coarse_ends[rows, :]

        @pl.when(sends_to(p))
        def _(p=p):
            jump_copy(p, 1).start()

    for p in range(PLACES):
        half_edge[p, 0:8] = half[pl.ds(p * CX, 8), :]
        half_edge[p, 8:16] = half[pl.ds(p * CX + CX - 8, 8), :]

    @pl.when(passes_on)
    def _():
        half_copies[1].start()

    def state_copy(n):
        return pltpu.make_async_remote_copy(
            chain.at[n], coarse.at[chip], chain_ss.at[n], chain_rs.at[chip],
            device_id=(n, space), device_id_type=MESH,
        )

    def state_arrival(p):
        return pltpu.make_async_remote_copy(
            chain.at[0], coarse.at[p], chain_ss.at[0], chain_rs.at[p],
            device_id=(tm, space), device_id_type=MESH,
        )

    @pl.when(is_owner)
    def _():
        jumps_mid[tm] = jump_mid[chip]
        jumps_edge[tm] = jump_edge[chip]

        def link(n, values):
            @pl.when(n != tm)
            def _():
                for i in range(2):
                    jump_arrival(n, i).wait_recv()

            own = jnp.concatenate(
                [jumps_edge[n, 0:8], jumps_mid[n], jumps_edge[n, 8:16]], axis=0
            )
            values = own + jnp.where(n > 0, 1.0, 0.0) * apply_coarse(chip, values)
            chain[n + 1] = values

            @pl.when(n + 1 != tm)
            def _():
                state_copy(n + 1).start()

            @pl.when(n + 1 == tm)
            def _():
                coarse[chip] = values

            return values

        lax.fori_loop(0, SLICES - 1, link, jnp.zeros((CX, TILE), F32))

    @pl.when(tm == 0)
    def _():
        coarse[...] = coarse_starts[...]

    place_of = [
        jnp.clip(sum(jnp.where(order[p] == t, p, 0) for p in range(PLACES)), 0, PLACES - 1)
        for t in range(PLACES)
    ]

    for p in range(PLACES):
        mean_place[p] = mean[pl.ds(p * CX, CX), :]

    for t in range(PLACES):
        at = place_of[t]
        half_out[t, 0:8] = half_edge[at, 0:8]
        half_out[t, 8 : CX - 8] = half_mid[at]
        half_out[t, CX - 8 : CX] = half_edge[at, 8:16]

    @pl.when(tm > 0)
    def _():
        for copy in half_copies:
            copy.wait_recv()
        for t in range(PLACES):
            at = place_of[t]
            for rows, difference, first, begin in (
                (slice(0, 8), prev_edge[at, 0:8], starts_edge, 0),
                (slice(8, CX - 8), prev_mid[at], starts, 0),
                (slice(CX - 8, CX), prev_edge[at, 8:16], starts_edge, 16),
            ):
                count = rows.stop - rows.start
                even_out[t, rows] = difference - first[t, pl.ds(begin, count, stride=2), :]
                odd_out[t, rows] = -difference - first[t, pl.ds(begin + 1, count, stride=2), :]

    for p in range(PLACES):
        @pl.when(jnp.logical_and(tm > 0, tm != 2 * p))
        def _(p=p):
            state_arrival(p).wait_recv()

    for t in range(PLACES):
        values = coarse[place_of[t]]
        coarse_out[t] = values
        sum_out[t] = apply_coarse(place_of[t], values) + mean_place[place_of[t]]

    for p in range(PLACES):
        @pl.when(sends_to(p))
        def _(p=p):
            for i in range(2):
                jump_copy(p, i).wait_send()

    @pl.when(passes_on)
    def _():
        for copy in half_copies:
            copy.wait_send()

    @pl.when(is_owner)
    def _():
        def sent(n, carry):
            @pl.when(n != tm)
            def _():
                state_copy(n).wait_send()

            return carry

        lax.fori_loop(1, SLICES, sent, 0)


def finish_kernel(
    sums, coarse, half, even_part, odd_part, ends_hbm, step_hbm, ends, step, store_sem
):
    later = lax.axis_index("tm") > 0
    even, odd = pl.ds(0, CX, stride=2), pl.ds(1, CX, stride=2)
    stores = []
    for t in range(PLACES):
        total, difference = sums[t], half[t]
        ends[t, even, :] = total + difference
        ends[t, odd, :] = total - difference
        stores.append(pltpu.make_async_copy(ends.at[t], ends_hbm.at[t], store_sem.at[0, t]))
        stores[-1].start()
        step[t, even, :] = jnp.where(later, coarse[t] + even_part[t], 0.0)
        step[t, odd, :] = jnp.where(later, coarse[t] + odd_part[t], 0.0)
        stores.append(pltpu.make_async_copy(step.at[t], step_hbm.at[t], store_sem.at[1, t]))
        stores[-1].start()
    for store in stores:
        store.wait()


def on_device(
    starts, diffusivity, velocity, obstacle, substep_scale, neighbors, coarse_x, coarse_y
):
    anywhere = pl.BlockSpec(memory_space=pltpu.HBM)
    vmem = pl.BlockSpec(memory_space=pltpu.VMEM)
    tiles = (PLACES, TILE, TILE)
    places = pltpu.VMEM((PLACES, CX, TILE), F32)
    dma = pltpu.SemaphoreType.DMA
    starts = starts[0]
    in_hbm = lambda x: pltpu.with_memory_space_constraint(x, pltpu.HBM)
    neighbors = neighbors.T
    parts = pl.pallas_call(
        fine_kernel,
        out_shape=(places,) * 5,
        in_specs=[anywhere] * 8,
        out_specs=(vmem,) * 5,
        scratch_shapes=[
            pltpu.SMEM((SUB,), F32),
            pltpu.SMEM((4, PLACES), jnp.int32),
            pltpu.VMEM((PLACES, 32, TILE), F32),
            pltpu.VMEM((PLACES, 32, TILE), F32),
            pltpu.VMEM((2, PLACES, 32, TILE), F32),
            pltpu.VMEM((PLACES, 32, TILE), jnp.int32),
            pltpu.VMEM((PLACES, TILE - 32, TILE), F32),
            pltpu.VMEM((PLACES, TILE - 32, TILE), F32),
            pltpu.VMEM((2, PLACES, TILE - 32, TILE), F32),
            pltpu.VMEM((PLACES, TILE - 32, TILE), jnp.int32),
            pltpu.VMEM((PLACES, CX, CX), F32),
            pltpu.VMEM(tiles, F32),
            dma((16,)),
            pltpu.VMEM((TILE * 8 + 8, TILE), F32),
            pltpu.VMEM((TILE * 8, TILE), F32),
            pltpu.VMEM((TILE * 8, TILE), F32),
            pltpu.VMEM((TILE * 8, TILE), F32),
            pltpu.VMEM((4, 2 * SUB, 8, TILE), F32),
            pltpu.VMEM((4, 2 * SUB, 8, TILE), F32),
            pltpu.VMEM((SUB, 2, 8, TILE), F32),
            pltpu.VMEM((SUB, 2, 8, TILE), F32),
            pltpu.VMEM((PLACES, CX, CX), BF16),
            pltpu.VMEM((PLACES, CX, CX), BF16),
            pltpu.VMEM(tiles, BF16),
            pltpu.VMEM(tiles, BF16),
            pltpu.VMEM((PLACES, CX, TILE), F32),
            pltpu.VMEM((PLACES * CX, TILE), F32),
            pltpu.VMEM((PLACES * CX, TILE), F32),
            pltpu.VMEM((PLACES * CX, TILE), F32),
            pltpu.VMEM((PLACES, MID, TILE), F32),
            pltpu.VMEM((PLACES, 16, TILE), F32),
            pltpu.VMEM((PLACES, MID, TILE), F32),
            pltpu.VMEM((PLACES, 16, TILE), F32),
            pltpu.VMEM((PLACES, MID, TILE), F32),
            pltpu.VMEM((PLACES, 16, TILE), F32),
            pltpu.VMEM((SLICES, MID, TILE), F32),
            pltpu.VMEM((SLICES, 16, TILE), F32),
            pltpu.VMEM((SLICES, CX, TILE), F32),
            pltpu.VMEM((PLACES, CX, TILE), F32),
            pltpu.VMEM((PLACES, CX, TILE), F32),
            dma((2,)),
            dma((2,)),
            dma((2, PLACES)),
            dma((2, SLICES)),
            dma((2,)),
            dma((2,)),
            dma((SLICES,)),
            dma((PLACES,)),
        ],
        compiler_params=pltpu.CompilerParams(
            collective_id=0, has_side_effects=True, vmem_limit_bytes=32 << 20
        ),
    )(*map(in_hbm, (substep_scale, neighbors, starts, diffusivity, velocity, obstacle, coarse_x, coarse_y)))
    ends, step = pl.pallas_call(
        finish_kernel,
        out_shape=(jax.ShapeDtypeStruct(tiles, F32),) * 2,
        in_specs=[vmem] * 5,
        out_specs=(anywhere, anywhere),
        scratch_shapes=[pltpu.VMEM(tiles, F32)] * 2 + [dma((2, PLACES))],
        compiler_params=pltpu.CompilerParams(vmem_limit_bytes=32 << 20),
    )(*parts)
    return ends[None], step[None]


def solution(mesh):
    placed = (
        P("tm", "space", None, None),
        P("space", None, None),
        P(None, "space", None, None),
        P("space", None, None),
        P(),
        P("space", None),
        P("space", None, None),
        P("space", None, None),
    )
    return jax.shard_map(
        on_device,
        mesh=mesh,
        in_specs=placed,
        out_specs=(P("tm", "space", None, None), P("tm", "space", None, None)),
        check_vma=False,
    )
```
